32 devices in a mesh: grp: 2 (over x), frame: 8 (over z, y), row: 2 (over core).
Axes of the slice: x: 2, y: 2, z: 4, core: 2. Of those that a mesh axis runs over, the one named last changes fastest.
Arguments:
- latents: float32 [4, 8, 16, 32, 16], P('grp', 'frame', 'row'), parts along dimension 0, may hold values from -6 to 6
- target_noise: float32 [4, 8, 16, 32, 16], P('grp', 'frame', 'row'), parts along dimension 0, may hold values from -6 to 6
- timesteps: int32 [4], P('grp'), parts along dimension 0, may hold values from 0 to 999
- patch_weight: bfloat16 [16, 1152], replicated, may hold values from -1.5 to 1.5
- time_weight: bfloat16 [256, 1152], replicated, may hold values from -0.5 to 0.5
- spatial_project: bfloat16 [1152, 1728], replicated
- spatial_output: bfloat16 [576, 1152], replicated, may hold values from -0.75 to 0.75
- temporal_project: bfloat16 [1152, 1728], replicated
- temporal_output: bfloat16 [576, 1152], replicated, may hold values from -0.75 to 0.75
- final_weight: bfloat16 [1152, 16], replicated, may hold values from -0.1875 to 0.1875
Outputs:
- errors: float32 [4, 8, 16, 32], P('grp', 'frame', 'row'), parts along dimension 0
The draws below stay inside these ranges and needn't reach their ends.
There are 2 independent parts, one for each index of `grp`. The reference program is written for one: setup_inputs(seed, part) draws one part's arguments, and reference() takes and returns one part's arrays. A program takes and returns all parts, laid end to end along the dimension named above; an argument that names none is the same for every part. Nothing has to cross between parts.
All inputs are finite; a program needn't handle non-finite values.
Results may differ from the reference program's by a relative error of at most 0.0045.
Values may be sent and summed in bfloat16 or wider, within the bound.
A program may use at most 128 MiB of HBM per device.

```python
import math
import jax
import jax.numpy as jnp
from jax import lax

D = 1152
HEAD_DIM = 72
HEADS = 8
CH = 16
TEMB = 256
STEPS = 1000
REACH = 2
WC = 32
B = 2
HD = 576
FRAMES = 8
ROWS = 16


def video_sample(key):
    sample = jax.random.normal(key, (B, FRAMES, ROWS, WC, CH), jnp.float32)
    return jnp.clip(sample, -6.0, 6.0)


def drawn_projection(key):
    keys_all = jax.random.split(key, 3)
    spread_factor = D ** (-0.5)
    query_weight = jax.random.normal(keys_all[0], (D, HD), jnp.float32) * spread_factor
    key_weight = jax.random.normal(keys_all[1], (D, HD), jnp.float32) * spread_factor
    value_weight = jax.random.normal(keys_all[2], (D, HD), jnp.float32) * spread_factor
    return jnp.concatenate([query_weight, key_weight, value_weight], axis=1).astype(jnp.bfloat16)


def draw_latents(key, part):
    return video_sample(jax.random.fold_in(key, 11))


def draw_target_noise(key, part):
    return video_sample(jax.random.fold_in(key, 23))


def draw_spatial_project(key, part):
    return drawn_projection(jax.random.fold_in(key, 31))


def draw_temporal_project(key, part):
    return drawn_projection(jax.random.fold_in(key, 47))


def normal_values(own_key, extent, width, bound, kind=jnp.bfloat16):
    return jnp.clip(width * jax.random.normal(own_key, extent, jnp.float32), -bound, bound).astype(kind)


def setup_inputs(seed: int = 0, part: int = 0) -> dict:
    keys = jax.random.split(jax.random.key(seed), 11)
    part_keys = jax.random.split(jax.random.fold_in(keys[10], part), 11)
    latents = draw_latents(jax.random.fold_in(jax.random.fold_in(keys[10], part), 71), part)
    target_noise = draw_target_noise(jax.random.fold_in(jax.random.fold_in(keys[10], part), 71), part)
    timesteps = jax.random.randint(part_keys[2], (B,), 0, STEPS).astype(jnp.int32)
    patch_weight = normal_values(keys[3], (CH, D), CH ** -0.5, 1.5)
    time_weight = normal_values(keys[4], (TEMB, D), (TEMB // 2) ** -0.5, 0.5)
    spatial_project = draw_spatial_project(jax.random.fold_in(keys[10], 71), part)
    spatial_output = normal_values(keys[6], (HD, D), (HD // 9) ** -0.5, 0.75)
    temporal_project = draw_temporal_project(jax.random.fold_in(keys[10], 71), part)
    temporal_output = normal_values(keys[8], (HD, D), (HD // 9) ** -0.5, 0.75)
    final_weight = normal_values(keys[9], (D, CH), D ** -0.5, 0.1875)
    return dict(latents=latents, target_noise=target_noise, timesteps=timesteps, patch_weight=patch_weight, time_weight=time_weight, spatial_project=spatial_project, spatial_output=spatial_output, temporal_project=temporal_project, temporal_output=temporal_output, final_weight=final_weight)


def to_wide(array):
    return lax.optimization_barrier(array).astype(jnp.float32)

def layer_norm(stream):
    average = lax.optimization_barrier(jnp.mean(stream, axis=-1, keepdims=True))
    centred = stream - average
    variance = lax.optimization_barrier(jnp.mean(centred * centred, axis=-1, keepdims=True))
    return centred * lax.rsqrt(variance + 1e-06)

def noise_levels(timesteps):
    counter = jnp.arange(STEPS, dtype=jnp.float32)
    betas_all = 0.0001 + (0.02 - 0.0001) * counter / (STEPS - 1)
    log_keep = jnp.cumsum(jnp.log1p(-betas_all))
    selector = (jnp.arange(STEPS, dtype=jnp.int32)[None, :] == timesteps.astype(jnp.int32)[:, None]).astype(jnp.float32)
    log_bar = jnp.dot(selector, log_keep, precision=lax.Precision.HIGHEST)
    kept_share = jnp.exp(log_bar)
    return (jnp.sqrt(kept_share), jnp.sqrt(1.0 - kept_share))

def time_embed(timesteps, time_weight):
    halfway = time_weight.shape[0] // 2
    freqs_all = jnp.exp(-math.log(10000.0) * jnp.arange(halfway, dtype=jnp.float32) / halfway)
    angles = timesteps.astype(jnp.float32)[:, None] * freqs_all[None, :]
    features = jnp.concatenate([jnp.cos(angles), jnp.sin(angles)], axis=-1).astype(jnp.bfloat16)
    return jnp.dot(features, time_weight, preferred_element_type=jnp.float32)

def softmax_rows(scores):
    row_top = lax.optimization_barrier(jnp.max(scores, axis=-1, keepdims=True))
    exponent = jnp.exp(scores - row_top)
    return (exponent / lax.optimization_barrier(jnp.sum(exponent, axis=-1, keepdims=True))).astype(jnp.bfloat16)

def spatial_attend(queries, padded, first_row, total_rows):
    batches, frames_n, rows_n, cols_n, inner_width = queries.shape
    window_rows = 2 * REACH + 1
    windows = jnp.concatenate([padded[:, :, offset:offset + rows_n] for offset in range(window_rows)], axis=3)
    heads_query = queries.reshape(batches, frames_n, rows_n, cols_n, HEADS, HEAD_DIM)
    key_part = windows[..., :inner_width].reshape(batches, frames_n, rows_n, window_rows * cols_n, HEADS, HEAD_DIM)
    value_part = windows[..., inner_width:].reshape(batches, frames_n, rows_n, window_rows * cols_n, HEADS, HEAD_DIM)
    scores = jnp.einsum('bfrqhe,bfrkhe->bfrhqk', to_wide(heads_query), to_wide(key_part), precision=lax.Precision.HIGHEST) / math.sqrt(HEAD_DIM)
    key_rows = first_row + jnp.arange(rows_n, dtype=jnp.int32)[:, None] + jnp.arange(window_rows * cols_n, dtype=jnp.int32)[None, :] // cols_n - REACH
    inside = (key_rows >= 0) & (key_rows < total_rows)
    scores = jnp.where(inside[None, None, :, None, None, :], scores, -1e+30)
    weights = softmax_rows(scores)
    mixed_out = jnp.einsum('bfrhqk,bfrkhe->bfrqhe', to_wide(weights), to_wide(value_part), precision=lax.Precision.HIGHEST)
    return mixed_out.astype(jnp.bfloat16).reshape(batches, frames_n, rows_n, cols_n, inner_width)

def temporal_attend(projected):
    batches, frames_n, places, triple = projected.shape
    inner_width = triple // 3
    shaped = projected.reshape(batches, frames_n, places, 3, HEADS, HEAD_DIM)
    scores = jnp.einsum('bfphe,bgphe->bphfg', to_wide(shaped[:, :, :, 0]), to_wide(shaped[:, :, :, 1]), precision=lax.Precision.HIGHEST) / math.sqrt(HEAD_DIM)
    weights = softmax_rows(scores)
    mixed_out = jnp.einsum('bphfg,bgphe->bfphe', to_wide(weights), to_wide(shaped[:, :, :, 2]), precision=lax.Precision.HIGHEST)
    return mixed_out.astype(jnp.bfloat16).reshape(batches, frames_n, places, inner_width)

def reference(latents, target_noise, timesteps, patch_weight, time_weight, spatial_project, spatial_output, temporal_project, temporal_output, final_weight):
    signal, spread = noise_levels(timesteps)
    noisy_input = (signal[:, None, None, None, None] * latents + spread[:, None, None, None, None] * target_noise).astype(jnp.bfloat16)
    time_vector = time_embed(timesteps, time_weight)
    stream = jnp.dot(noisy_input, patch_weight, preferred_element_type=jnp.float32) + time_vector[:, None, None, None, :]
    batches, frames_n, rows_n, cols_n, model_width = stream.shape
    inner_width = spatial_output.shape[0]
    normed = layer_norm(stream).astype(jnp.bfloat16)
    projected = jnp.dot(normed, spatial_project, preferred_element_type=jnp.float32).astype(jnp.bfloat16)
    padded = jnp.pad(projected[..., inner_width:], ((0, 0), (0, 0), (REACH, REACH), (0, 0), (0, 0)))
    mixed_out = spatial_attend(projected[..., :inner_width], padded, 0, ROWS)
    stream = stream + jnp.dot(mixed_out, spatial_output, preferred_element_type=jnp.float32)
    normed = layer_norm(stream).astype(jnp.bfloat16).reshape(batches, frames_n, rows_n * cols_n, model_width)
    projected = jnp.dot(normed, temporal_project, preferred_element_type=jnp.float32).astype(jnp.bfloat16)
    mixed_out = temporal_attend(projected)
    temporal_delta = jnp.dot(mixed_out, temporal_output, preferred_element_type=jnp.float32)
    stream = stream + temporal_delta.reshape(stream.shape)
    normed = layer_norm(stream).astype(jnp.bfloat16)
    predicted = jnp.dot(normed, final_weight, preferred_element_type=jnp.float32)
    residual_gap = predicted - target_noise
    return lax.optimization_barrier(jnp.mean(residual_gap * residual_gap, axis=-1))
```

```python
import math

import jax
import jax.numpy as jnp
from jax import lax
from jax.sharding import PartitionSpec as P

HEAD_DIM = 72
HEADS = 8
STEPS = 1000
REACH = 2
HI = lax.Precision.HIGHEST
F32 = jnp.float32


def noise_levels(timesteps):
    counter = jnp.arange(STEPS, dtype=F32)
    betas_all = 0.0001 + (0.02 - 0.0001) * counter / (STEPS - 1)
    log_keep = jnp.cumsum(jnp.log1p(-betas_all))
    selector = (jnp.arange(STEPS, dtype=jnp.int32)[None, :] == timesteps[:, None]).astype(F32)
    log_bar = jnp.dot(selector, log_keep, precision=HI)
    kept_share = jnp.exp(log_bar)
    return (jnp.sqrt(kept_share), jnp.sqrt(1.0 - kept_share))


def time_embed(timesteps, time_weight):
    halfway = time_weight.shape[0] // 2
    freqs_all = jnp.exp(-math.log(10000.0) * jnp.arange(halfway, dtype=F32) / halfway)
    angles = timesteps.astype(F32)[:, None] * freqs_all[None, :]
    features = jnp.concatenate([jnp.cos(angles), jnp.sin(angles)], axis=-1).astype(jnp.bfloat16)
    return jnp.dot(features, time_weight, preferred_element_type=F32)


def pieces(value, count):
    parts = []
    for _ in range(count):
        part = value.astype(jnp.bfloat16)
        parts.append(part)
        value = value - part.astype(F32)
    return parts


def wide_dot(value, weight, count=2):
    rows = value.shape[0]
    out = jnp.dot(jnp.concatenate(pieces(value, count), axis=0), weight, preferred_element_type=F32)
    return sum(out[i * rows : (i + 1) * rows] for i in range(count))


def centre(value):
    return value - jnp.mean(value, axis=-1, keepdims=True)


def local(
    latents,
    target_noise,
    timesteps,
    patch_weight,
    time_weight,
    spatial_project,
    spatial_output,
    temporal_project,
    temporal_output,
    final_weight,
):
    batches, frames_l, rows_l, cols, ch = latents.shape
    peers, halves = lax.axis_size("frame"), lax.axis_size("row")
    fi, gi = lax.axis_index("frame"), lax.axis_index("row")
    frames, rows = frames_l * peers, rows_l * halves
    places = rows_l * cols // peers
    q_rows, q_cols = max(1, places // cols), min(cols, places)
    width = patch_weight.shape[1]
    inner = spatial_output.shape[0]
    scale = 1.0 / math.sqrt(HEAD_DIM)

    signal, spread = noise_levels(timesteps)
    noisy = (
        signal[:, None, None, None, None] * latents
        + spread[:, None, None, None, None] * target_noise
    ).astype(jnp.bfloat16)
    time_vector = time_embed(timesteps, time_weight)

    whole = lax.all_gather(
        noisy.reshape(batches, frames_l, rows_l, cols * ch), ("frame", "row"), axis=0, tiled=False
    )
    whole = whole.reshape(peers, halves, batches, frames_l, rows_l, cols * ch)
    whole = whole.transpose(2, 0, 3, 1, 4, 5).reshape(batches, frames, rows, cols * ch)
    target = lax.all_to_all(
        target_noise.reshape(batches, frames_l, peers, places * ch),
        "frame",
        split_axis=2,
        concat_axis=1,
        tiled=True,
    ).reshape(batches * frames * places, ch)

    first = gi * rows_l + (fi * places) // cols
    column = (fi * places) % cols
    k_rows = q_rows + 2 * REACH
    padded = jnp.pad(whole, ((0, 0), (0, 0), (REACH, REACH), (0, 0)))
    near = lax.dynamic_slice_in_dim(padded, first, k_rows, axis=2).reshape(
        batches, frames, k_rows, cols, ch
    )
    own = lax.dynamic_slice_in_dim(near[:, :, REACH : REACH + q_rows], column, q_cols, axis=3)

    base = jnp.concatenate([patch_weight.astype(F32), time_vector], axis=0)
    base_c = centre(base)
    feats = base.shape[0]
    spatial = wide_dot(base_c, spatial_project, 3).reshape(feats, 3, HEADS, HEAD_DIM)
    mixer = jnp.einsum("ahe,bhe->hab", spatial[:, 0], spatial[:, 1], precision=HI) * scale
    out_heads = spatial_output.reshape(HEADS, HEAD_DIM, width).astype(F32)
    carried = jnp.einsum("ahe,hed->had", spatial[:, 2], out_heads, precision=HI)
    full_c = jnp.concatenate([base_c, centre(carried).reshape(HEADS * feats, width)], axis=0)
    temporal = wide_dot(full_c, temporal_project, 2)

    def lifted(tokens):
        mark = jnp.broadcast_to(
            jnp.eye(batches, dtype=F32)[:, None, None, None, :], tokens.shape[:-1] + (batches,)
        )
        return jnp.concatenate([tokens.astype(F32), mark], axis=-1)

    def scaled(tokens):
        stream = jnp.einsum("bfrca,ad->bfrcd", tokens, base_c, precision=HI)
        return tokens * lax.rsqrt(jnp.mean(stream * stream, axis=-1, keepdims=True) + 1e-06)

    near_l, own_l = lifted(near), lifted(own)
    keys = scaled(near_l).reshape(batches, frames, k_rows * cols, feats)
    query = scaled(own_l).reshape(batches, frames, places, feats)
    query = jnp.einsum("bfqa,hac->bfhqc", query, mixer, precision=HI)
    scores = jnp.einsum("bfhqc,bfkc->bfhqk", query, keys, precision=HI)
    key_row = jnp.arange(k_rows * cols, dtype=jnp.int32) // cols
    query_row = jnp.arange(places, dtype=jnp.int32) // q_cols
    off = key_row[None, :] - query_row[:, None]
    there = first + key_row - REACH
    inside = ((off >= 0) & (off <= 2 * REACH)) & ((there >= 0) & (there < rows))[None, :]
    scores = jnp.where(inside, scores, -1e30)
    exponent = jnp.exp(scores - jnp.max(scores, axis=-1, keepdims=True))
    weights = exponent / jnp.sum(exponent, axis=-1, keepdims=True)
    mixed = jnp.einsum("bfhqk,bfkc->bfqhc", weights, keys, precision=HI)
    tokens = batches * frames * places
    state = jnp.concatenate(
        [own_l.reshape(tokens, feats), mixed.reshape(tokens, HEADS * feats)], axis=-1
    )

    stream = jnp.dot(state, full_c, precision=HI)
    share = lax.rsqrt(jnp.mean(stream * stream, axis=-1, keepdims=True) + 1e-06)
    projected = (jnp.dot(state, temporal, precision=HI) * share).astype(jnp.bfloat16)
    shaped = projected.reshape(batches, frames, places, 3, HEADS, HEAD_DIM)
    scores = (
        jnp.einsum(
            "bfphe,bgphe->bphfg", shaped[:, :, :, 0], shaped[:, :, :, 1], preferred_element_type=F32
        )
        * scale
    )
    exponent = jnp.exp(scores - jnp.max(scores, axis=-1, keepdims=True))
    weights = (exponent / jnp.sum(exponent, axis=-1, keepdims=True)).astype(jnp.bfloat16)
    mixed = (
        jnp.einsum("bphfg,bgphe->bfphe", weights, shaped[:, :, :, 2], preferred_element_type=F32)
        .astype(jnp.bfloat16)
        .reshape(tokens, inner)
    )
    stream = stream + jnp.dot(mixed, temporal_output, preferred_element_type=F32)
    stream = centre(stream)
    share = lax.rsqrt(jnp.mean(stream * stream, axis=-1, keepdims=True) + 1e-06)
    predicted = jnp.dot(
        (stream * share).astype(jnp.bfloat16), final_weight, preferred_element_type=F32
    )
    gap = predicted - target
    errors = jnp.mean(gap * gap, axis=-1).reshape(batches, frames, places)
    errors = lax.all_to_all(errors, "frame", split_axis=1, concat_axis=2, tiled=True)
    return errors.reshape(batches, frames_l, rows_l, cols)


def solution(mesh):
    data = P("grp", "frame", "row", None, None)
    return jax.shard_map(
        local,
        mesh=mesh,
        in_specs=(data, data, P("grp")) + (P(),) * 7,
        out_specs=P("grp", "frame", "row", None),
        check_vma=False,
    )
```

```python
import functools
import math

import jax
import jax.numpy as jnp
from jax import lax
from jax.experimental import pallas as pl
from jax.experimental.pallas import tpu as pltpu
from jax.sharding import PartitionSpec as P

HEAD_DIM = 72
HEADS = 8
STEPS = 1000
REACH = 2
HI = lax.Precision.HIGHEST
F32 = jnp.float32
MESH = pl.DeviceIdType.MESH


def noise_levels(timesteps):
    counter = jnp.arange(STEPS, dtype=F32)
    betas_all = 0.0001 + (0.02 - 0.0001) * counter / (STEPS - 1)
    log_keep = jnp.cumsum(jnp.log1p(-betas_all))
    selector = (jnp.arange(STEPS, dtype=jnp.int32)[None, :] == timesteps[:, None]).astype(F32)
    log_bar = jnp.dot(selector, log_keep, precision=HI)
    kept_share = jnp.exp(log_bar)
    return (jnp.sqrt(kept_share), jnp.sqrt(1.0 - kept_share))


def time_embed(timesteps, time_weight):
    halfway = time_weight.shape[0] // 2
    freqs_all = jnp.exp(-math.log(10000.0) * jnp.arange(halfway, dtype=F32) / halfway)
    angles = timesteps.astype(F32)[:, None] * freqs_all[None, :]
    features = jnp.concatenate([jnp.cos(angles), jnp.sin(angles)], axis=-1).astype(jnp.bfloat16)
    return jnp.dot(features, time_weight, preferred_element_type=F32)


def pieces(value, count):
    parts = []
    for _ in range(count):
        part = value.astype(jnp.bfloat16)
        parts.append(part)
        value = value - part.astype(F32)
    return parts


def wide_dot(value, weight, count=2):
    rows = value.shape[0]
    out = jnp.dot(jnp.concatenate(pieces(value, count), axis=0), weight, preferred_element_type=F32)
    return sum(out[i * rows : (i + 1) * rows] for i in range(count))


def centre(value):
    return value - jnp.mean(value, axis=-1, keepdims=True)


def local(
    latents,
    target_noise,
    timesteps,
    patch_weight,
    time_weight,
    spatial_project,
    spatial_output,
    temporal_project,
    temporal_output,
    final_weight,
):
    batches, frames_l, rows_l, cols, ch = latents.shape
    peers, halves = lax.axis_size("frame"), lax.axis_size("row")
    fi, gi = lax.axis_index("frame"), lax.axis_index("row")
    frames, rows = frames_l * peers, rows_l * halves
    places = rows_l * cols // peers
    q_rows, q_cols = max(1, places // cols), min(cols, places)
    width = patch_weight.shape[1]
    inner = spatial_output.shape[0]
    scale = 1.0 / math.sqrt(HEAD_DIM)

    signal, spread = noise_levels(timesteps)
    noisy = (
        signal[:, None, None, None, None] * latents
        + spread[:, None, None, None, None] * target_noise
    ).astype(jnp.bfloat16)
    time_vector = time_embed(timesteps, time_weight)

    whole = lax.all_gather(
        noisy.reshape(batches, frames_l, rows_l, cols * ch), ("frame", "row"), axis=0, tiled=False
    )
    whole = whole.reshape(peers, halves, batches, frames_l, rows_l, cols * ch)
    whole = whole.transpose(2, 0, 3, 1, 4, 5).reshape(batches, frames, rows, cols * ch)
    target = lax.all_to_all(
        target_noise.reshape(batches, frames_l, peers, places * ch),
        "frame",
        split_axis=2,
        concat_axis=1,
        tiled=True,
    ).reshape(batches * frames * places, ch)

    first = gi * rows_l + (fi * places) // cols
    column = (fi * places) % cols
    k_rows = q_rows + 2 * REACH
    padded = jnp.pad(whole, ((0, 0), (0, 0), (REACH, REACH), (0, 0)))
    near = lax.dynamic_slice_in_dim(padded, first, k_rows, axis=2).reshape(
        batches, frames, k_rows, cols, ch
    )
    own = lax.dynamic_slice_in_dim(near[:, :, REACH : REACH + q_rows], column, q_cols, axis=3)

    base = jnp.concatenate([patch_weight.astype(F32), time_vector], axis=0)
    base_c = centre(base)
    feats = base.shape[0]
    spatial = wide_dot(base_c, spatial_project, 3).reshape(feats, 3, HEADS, HEAD_DIM)
    mixer = jnp.einsum("ahe,bhe->hab", spatial[:, 0], spatial[:, 1], precision=HI) * scale
    out_heads = spatial_output.reshape(HEADS, HEAD_DIM, width).astype(F32)
    carried = jnp.einsum("ahe,hed->had", spatial[:, 2], out_heads, precision=HI)
    full_c = jnp.concatenate([base_c, centre(carried).reshape(HEADS * feats, width)], axis=0)
    temporal = wide_dot(full_c, temporal_project, 2)

    def lifted(tokens):
        mark = jnp.broadcast_to(
            jnp.eye(batches, dtype=F32)[:, None, None, None, :], tokens.shape[:-1] + (batches,)
        )
        return jnp.concatenate([tokens.astype(F32), mark], axis=-1)

    def scaled(tokens):
        stream = jnp.einsum("bfrca,ad->bfrcd", tokens, base_c, precision=HI)
        return tokens * lax.rsqrt(jnp.mean(stream * stream, axis=-1, keepdims=True) + 1e-06)

    near_l, own_l = lifted(near), lifted(own)
    keys = scaled(near_l).reshape(batches, frames, k_rows * cols, feats)
    query = scaled(own_l).reshape(batches, frames, places, feats)
    query = jnp.einsum("bfqa,hac->bfhqc", query, mixer, precision=HI)
    scores = jnp.einsum("bfhqc,bfkc->bfhqk", query, keys, precision=HI)
    key_row = jnp.arange(k_rows * cols, dtype=jnp.int32) // cols
    query_row = jnp.arange(places, dtype=jnp.int32) // q_cols
    off = key_row[None, :] - query_row[:, None]
    there = first + key_row - REACH
    inside = ((off >= 0) & (off <= 2 * REACH)) & ((there >= 0) & (there < rows))[None, :]
    scores = jnp.where(inside, scores, -1e30)
    exponent = jnp.exp(scores - jnp.max(scores, axis=-1, keepdims=True))
    weights = exponent / jnp.sum(exponent, axis=-1, keepdims=True)
    mixed = jnp.einsum("bfhqk,bfkc->bfqhc", weights, keys, precision=HI)
    tokens = batches * frames * places
    state = jnp.concatenate(
        [own_l.reshape(tokens, feats), mixed.reshape(tokens, HEADS * feats)], axis=-1
    )

    stream = jnp.dot(state, full_c, precision=HI)
    share = lax.rsqrt(jnp.mean(stream * stream, axis=-1, keepdims=True) + 1e-06)
    projected = (jnp.dot(state, temporal, precision=HI) * share).astype(jnp.bfloat16)
    shaped = projected.reshape(batches, frames, places, 3, HEADS, HEAD_DIM)
    scores = (
        jnp.einsum(
            "bfphe,bgphe->bphfg", shaped[:, :, :, 0], shaped[:, :, :, 1], preferred_element_type=F32
        )
        * scale
    )
    exponent = jnp.exp(scores - jnp.max(scores, axis=-1, keepdims=True))
    weights = (exponent / jnp.sum(exponent, axis=-1, keepdims=True)).astype(jnp.bfloat16)
    mixed = (
        jnp.einsum("bphfg,bgphe->bfphe", weights, shaped[:, :, :, 2], preferred_element_type=F32)
        .astype(jnp.bfloat16)
        .reshape(tokens, inner)
    )
    stream = stream + jnp.dot(mixed, temporal_output, preferred_element_type=F32)
    stream = centre(stream)
    share = lax.rsqrt(jnp.mean(stream * stream, axis=-1, keepdims=True) + 1e-06)
    predicted = jnp.dot(
        (stream * share).astype(jnp.bfloat16), final_weight, preferred_element_type=F32
    )
    gap = predicted - target
    errors = jnp.mean(gap * gap, axis=-1).reshape(batches, frames, places)
    errors = lax.all_to_all(errors, "frame", split_axis=1, concat_axis=2, tiled=True)
    return errors.reshape(batches, frames_l, rows_l, cols)


def split2(value):
    high = value.astype(jnp.bfloat16)
    return high, (value - high.astype(F32)).astype(jnp.bfloat16)


def dot(a, b, axes=((1,), (0,)), precision=None):
    return lax.dot_general(a, b, (axes, ((), ())), precision=precision, preferred_element_type=F32)


NT = ((1,), (1,))


def fused_kernel(
    peers,
    halves,
    batches,
    cols,
    x_ref,
    target_ref,
    base_ref,
    final_ref,
    sp_hbm,
    so_hbm,
    tp_hbm,
    to_hbm,
    out_ref,
    sp,
    so,
    tp,
    to,
    w_sem,
    near,
    goal,
    err_out,
    err_in,
    mall,
    full_hi,
    full_lo,
    gram,
    gt_hi,
    gt_lo,
    state,
    qkv,
    mixed_t,
    x_send,
    x_recv,
    h_send,
    h_recv,
    t_send,
    t_recv,
    e_send,
    e_recv,
):
    rows_l, ch, lanes = x_ref.shape
    per = batches * cols
    pair = lanes // per
    width = base_ref.shape[1]
    inner = so.shape[0]
    feats = base_ref.shape[0]
    window = 2 * REACH + 1
    fi, gi = lax.axis_index("frame"), lax.axis_index("row")
    weight_copies = [
        pltpu.make_async_copy(src, dst, w_sem.at[i])
        for i, (src, dst) in enumerate(((sp_hbm, sp), (so_hbm, so), (tp_hbm, tp), (to_hbm, to)))
    ]
    for copy in weight_copies:
        copy.start()

    barrier = pltpu.get_barrier_semaphore()
    for df in range(peers):
        for dg in range(halves):
            if df or dg:
                pl.semaphore_signal(
                    barrier,
                    inc=1,
                    device_id={
                        "frame": lax.rem(fi + df, peers),
                        "row": lax.rem(gi + dg, halves),
                    },
                    device_id_type=MESH,
                )
    pl.semaphore_wait(barrier, peers * halves - 1)

    def start_of(place):
        return jnp.clip(place - REACH, 0, rows_l - window)

    def x_copy(peer):
        return pltpu.make_async_remote_copy(
            src_ref=x_ref.at[pl.ds(start_of(peer), window)],
            dst_ref=near.at[fi, pl.ds(0, window)],
            send_sem=x_send.at[peer],
            recv_sem=x_recv.at[fi],
            device_id={"frame": peer, "row": gi},
            device_id_type=MESH,
        )

    def t_copy(peer):
        return pltpu.make_async_remote_copy(
            src_ref=target_ref.at[peer],
            dst_ref=goal.at[fi],
            send_sem=t_send.at[peer],
            recv_sem=t_recv.at[fi],
            device_id={"frame": peer, "row": gi},
            device_id_type=MESH,
        )

    def halo_copy(slot, peer, half, first):
        return pltpu.make_async_remote_copy(
            src_ref=x_ref.at[pl.ds(first, REACH)],
            dst_ref=near.at[fi, pl.ds(window, REACH)],
            send_sem=h_send.at[slot],
            recv_sem=h_recv.at[fi],
            device_id={"frame": peer, "row": half},
            device_id_type=MESH,
        )

    def halos(action):
        for i in range(REACH):

            @pl.when(gi < halves - 1)
            def _():
                action(halo_copy(i, i, gi + 1, rows_l - REACH))

            @pl.when(gi > 0)
            def _():
                action(halo_copy(REACH + i, peers - REACH + i, gi - 1, 0))

    halos(lambda copy: copy.start())
    for k in range(1, peers):
        x_copy(lax.rem(fi + k, peers)).start()
    for k in range(1, peers):
        t_copy(lax.rem(fi + k, peers)).start()
    near[fi, 0:window] = x_ref[pl.ds(start_of(fi), window)]
    goal[fi] = target_ref[fi]
    takes_halo = ((fi < REACH) & (gi > 0)) | ((fi >= peers - REACH) & (gi < halves - 1))

    @pl.when(jnp.logical_not(takes_halo))
    def _():
        near[:, window:] = jnp.zeros((peers, REACH, ch, lanes), near.dtype)

    base = base_ref[...]
    base_c = base - jnp.mean(base, axis=-1, keepdims=True)
    b1, b2 = split2(base_c)
    b3 = (base_c - b1.astype(F32) - b2.astype(F32)).astype(jnp.bfloat16)
    weight_copies[0].wait()
    wide = dot(jnp.concatenate([b1, b2, b3], axis=0), sp[...])
    spatial = wide[:feats] + wide[feats : 2 * feats] + wide[2 * feats :]
    sq, sk, sv = (spatial[:, i * inner : (i + 1) * inner] for i in range(3))
    owner = lax.broadcasted_iota(jnp.int32, (feats, inner), 1) // HEAD_DIM

    def by_head(value):
        return jnp.concatenate(
            [jnp.where(owner == h, value, 0.0) for h in range(HEADS)], axis=0
        )

    sk3 = jnp.concatenate([sk] * 3 + [jnp.zeros((128 - 3 * feats, inner), F32)], axis=0)
    mixer = dot(by_head(sq), sk3, NT, HI) * (1.0 / math.sqrt(HEAD_DIM))
    for h in range(HEADS):
        mall[:, h * 128 : (h + 1) * 128] = mixer[h * feats : (h + 1) * feats]
    v1, v2 = split2(by_head(sv))
    weight_copies[1].wait()
    carried = dot(v1, so[...]) + dot(v2, so[...])
    carried = carried - jnp.mean(carried, axis=-1, keepdims=True)
    rest = state.shape[0] - feats * (HEADS + 1)
    full = jnp.concatenate([base_c, carried, jnp.zeros((rest, width), F32)], axis=0)
    f1, f2 = split2(full)
    full_hi[...] = f1
    full_lo[...] = f2
    gram[...] = (dot(f1, f1, NT) + dot(f1, f2, NT) + dot(f2, f1, NT)) * (1.0 / width)
    weight_copies[2].wait()
    g1, g2 = split2((dot(f1, tp[...]) + dot(f2, tp[...])).T)
    gt_hi[...] = g1
    gt_lo[...] = g2
    small = dot(base_c, base_c, NT, HI) * (1.0 / width)

    for k in range(1, peers):
        x_copy(lax.rem(fi + k, peers)).wait_send()
        pltpu.make_async_remote_copy(
            src_ref=x_ref.at[pl.ds(0, window)],
            dst_ref=near.at[lax.rem(fi + k, peers), pl.ds(0, window)],
            send_sem=x_send.at[fi],
            recv_sem=x_recv.at[lax.rem(fi + k, peers)],
            device_id={"frame": lax.rem(fi + k, peers), "row": gi},
            device_id_type=MESH,
        ).wait_recv()
    halos(lambda copy: copy.wait_send())

    @pl.when(takes_halo)
    def _():
        for k in range(peers):
            pltpu.make_async_remote_copy(
                src_ref=x_ref.at[pl.ds(0, REACH)],
                dst_ref=near.at[k, pl.ds(window, REACH)],
                send_sem=h_send.at[0],
                recv_sem=h_recv.at[k],
                device_id={"frame": k, "row": lax.rem(gi + 1, halves)},
                device_id_type=MESH,
            ).wait_recv()

    mark = (
        lax.broadcasted_iota(jnp.int32, (feats - ch, lanes), 1) // cols
        == lax.broadcasted_iota(jnp.int32, (feats - ch, lanes), 0)
    ).astype(F32)
    spots, biases = [], []
    for d in range(-REACH, REACH + 1):
        lr = fi + d
        spots.append(
            jnp.where(
                lr < 0,
                window + lr + REACH,
                jnp.where(lr >= rows_l, window + lr - rows_l, lr - start_of(fi)),
            )
        )
        there = gi * rows_l + lr
        biases.append(jnp.where((there >= 0) & (there < rows_l * halves), 0.0, -1e30).astype(F32))

    tiles_of_u = []
    for f in range(peers):
        lifted = jnp.concatenate(
            [
                jnp.concatenate([near[f, spot].astype(F32), mark], axis=0)
                for spot in spots
            ],
            axis=1,
        )
        var = jnp.sum(lifted * dot(small, lifted, precision=HI), axis=0, keepdims=True)
        y = lifted * lax.rsqrt(jnp.maximum(var, 0.0) + 1e-06)
        high = y.astype(jnp.bfloat16).astype(F32)
        keys3 = jnp.concatenate(
            [high, y - high, high, jnp.zeros((128 - 3 * feats, window * lanes), F32)], axis=0
        )
        keys3 = [keys3[:, i * lanes : (i + 1) * lanes].T for i in range(window)]
        own = y[:, REACH * lanes : (REACH + 1) * lanes].T[:per]
        ask = dot(own, mall[...], precision=HI)
        lead = ask.astype(jnp.bfloat16).astype(F32)
        lane = lax.broadcasted_iota(jnp.int32, ask.shape, 1) % 128
        ask3 = jnp.where(lane < 2 * feats, lead, ask - lead).astype(jnp.bfloat16)
        state[0:feats, f * per : (f + 1) * per] = lifted[
            :, REACH * lanes : REACH * lanes + per
        ]
        for b in range(batches):
            cut = slice(b * cols, (b + 1) * cols)
            k3 = jnp.concatenate([k[cut] for k in keys3], axis=0).astype(jnp.bfloat16)
            q3 = jnp.concatenate(
                [ask3[cut, h * 128 : (h + 1) * 128] for h in range(HEADS)], axis=0
            )
            scores = dot(k3, q3, NT)
            scores = jnp.concatenate(
                [scores[i * cols : (i + 1) * cols] + biases[i] for i in range(window)], axis=0
            )
            weight = jnp.exp(scores - jnp.max(scores, axis=0, keepdims=True))
            weight = weight * (1.0 / jnp.sum(weight, axis=0, keepdims=True))
            both = dot(k3, weight.astype(jnp.bfloat16), ((0,), (0,)))
            tiles_of_u.append(both[:feats] + both[feats : 2 * feats])
    for h in range(HEADS):
        state[feats * (h + 1) : feats * (h + 2), :] = jnp.concatenate(
            [u[:, h * cols : (h + 1) * cols] for u in tiles_of_u], axis=1
        )
    state[feats * (HEADS + 1) :, :] = jnp.zeros((rest, state.shape[1]), F32)

    z = state[...]
    z1, z2 = split2(z)
    var = jnp.sum(z * (dot(gram[...], z, precision=HI)), axis=0, keepdims=True)
    share = lax.rsqrt(jnp.maximum(var, 0.0) + 1e-06)
    qkv[...] = (dot(gt_hi[...], z1) + dot(gt_hi[...], z2) + dot(gt_lo[...], z1)) * share
    tiles = peers // pair
    scale = 1.0 / math.sqrt(HEAD_DIM)

    def tile_of(part, h, t):
        top = part * inner + h * HEAD_DIM
        return qkv[top : top + HEAD_DIM, t * lanes : (t + 1) * lanes]

    def turned(value, s):
        return pltpu.roll(value, s * per, 1) if s else value

    for h in range(HEADS):
        ks = [turned(tile_of(1, h, t), s) for t in range(tiles) for s in range(pair)]
        vs = [turned(tile_of(2, h, t), s) for t in range(tiles) for s in range(pair)]
        for p in range(tiles):
            q = tile_of(0, h, p) * scale
            logits = [jnp.sum(q * k, axis=0, keepdims=True) for k in ks]
            top = functools.reduce(jnp.maximum, logits)
            exps = [jnp.exp(s - top) for s in logits]
            total = 1.0 / functools.reduce(jnp.add, exps)
            acc = functools.reduce(
                jnp.add, [(e * total) * v for e, v in zip(exps, vs)]
            )
            mixed_t[h * HEAD_DIM : (h + 1) * HEAD_DIM, p * lanes : (p + 1) * lanes] = acc

    zt = z.T
    zt1, zt2 = split2(zt)
    weight_copies[3].wait()
    stream = dot(zt1, full_hi[...]) + dot(zt2, full_hi[...]) + dot(zt1, full_lo[...])
    stream = stream + dot(mixed_t[...].T.astype(jnp.bfloat16), to[...])
    stream = stream - jnp.mean(stream, axis=-1, keepdims=True)
    share = lax.rsqrt(jnp.mean(stream * stream, axis=-1, keepdims=True) + 1e-06)
    predicted = dot(final_ref[...], (stream * share).astype(jnp.bfloat16), NT)

    for k in range(1, peers):
        t_copy(lax.rem(fi + k, peers)).wait_send()
        pltpu.make_async_remote_copy(
            src_ref=target_ref.at[0],
            dst_ref=goal.at[lax.rem(fi + k, peers)],
            send_sem=t_send.at[fi],
            recv_sem=t_recv.at[lax.rem(fi + k, peers)],
            device_id={"frame": lax.rem(fi + k, peers), "row": gi},
            device_id_type=MESH,
        ).wait_recv()
    aim = jnp.concatenate([goal[f][:, :per] for f in range(peers)], axis=1)
    gap = predicted - aim
    errors = jnp.mean(gap * gap, axis=0, keepdims=True)
    for t in range(tiles):
        err_out[t] = jnp.broadcast_to(errors[:, t * lanes : (t + 1) * lanes], (8, lanes))

    def e_copy(peer, source, other):
        return pltpu.make_async_remote_copy(
            src_ref=err_out.at[peer // pair],
            dst_ref=err_in.at[source],
            send_sem=e_send.at[peer],
            recv_sem=e_recv.at[source],
            device_id={"frame": other, "row": gi},
            device_id_type=MESH,
        )

    for k in range(1, peers):
        e_copy(lax.rem(fi + k, peers), fi, lax.rem(fi + k, peers)).start()
    err_in[fi] = err_out[fi // pair]
    for k in range(1, peers):
        other = lax.rem(fi + k, peers)
        e_copy(other, fi, other).wait_send()
        e_copy(fi, other, other).wait_recv()
    got = jnp.concatenate([err_in[k, 0:1] for k in range(peers)], axis=0)
    result = got[:, :per]
    for s in range(1, pair):
        result = jnp.where(lax.rem(fi, pair) == s, got[:, s * per : (s + 1) * per], result)
    out_ref[...] = result


def fused(
    latents,
    target_noise,
    timesteps,
    patch_weight,
    time_weight,
    spatial_project,
    spatial_output,
    temporal_project,
    temporal_output,
    final_weight,
):
    batches, _, rows_l, cols, ch = latents.shape
    peers, halves = lax.axis_size("frame"), lax.axis_size("row")
    width, inner = patch_weight.shape[1], spatial_output.shape[0]
    per, lanes = batches * cols, 128
    signal, spread = noise_levels(timesteps)
    noisy = (
        signal[:, None, None, None, None] * latents
        + spread[:, None, None, None, None] * target_noise
    ).astype(jnp.bfloat16)

    def channel_major(value):
        value = value[:, 0].transpose(1, 3, 0, 2).reshape(rows_l, ch, per)
        return jnp.pad(value, ((0, 0), (0, 0), (0, lanes - per)))

    feats = -(-(ch + batches) // 8) * 8
    time_vector = time_embed(timesteps, time_weight)
    base = jnp.concatenate(
        [
            patch_weight.astype(F32),
            time_vector,
            jnp.zeros((feats - ch - batches, width), F32),
        ],
        axis=0,
    )
    tokens = peers * per
    depth = -(-(feats * (HEADS + 1)) // 128) * 128
    bf16 = jnp.bfloat16
    vmem, anywhere = pl.BlockSpec(memory_space=pltpu.VMEM), pl.BlockSpec(memory_space=pl.ANY)
    sems = pltpu.SemaphoreType.DMA
    out = pl.pallas_call(
        functools.partial(fused_kernel, peers, halves, batches, cols),
        out_shape=jax.ShapeDtypeStruct((rows_l, per), F32),
        in_specs=[vmem] * 4 + [anywhere] * 4,
        out_specs=vmem,
        scratch_shapes=[
            pltpu.VMEM(spatial_project.shape, bf16),
            pltpu.VMEM(spatial_output.shape, bf16),
            pltpu.VMEM(temporal_project.shape, bf16),
            pltpu.VMEM(temporal_output.shape, bf16),
            sems((4,)),
            pltpu.VMEM((peers, 3 * REACH + 1, ch, lanes), bf16),
            pltpu.VMEM((peers, ch, lanes), F32),
            pltpu.VMEM((tokens // lanes, 8, lanes), F32),
            pltpu.VMEM((peers, 8, lanes), F32),
            pltpu.VMEM((feats, HEADS * 128), F32),
            pltpu.VMEM((depth, width), bf16),
            pltpu.VMEM((depth, width), bf16),
            pltpu.VMEM((depth, depth), F32),
            pltpu.VMEM((3 * inner, depth), bf16),
            pltpu.VMEM((3 * inner, depth), bf16),
            pltpu.VMEM((depth, tokens), F32),
            pltpu.VMEM((3 * inner, tokens), F32),
            pltpu.VMEM((inner, tokens), F32),
            sems((peers,)),
            sems((peers,)),
            sems((2 * REACH,)),
            sems((peers,)),
            sems((peers,)),
            sems((peers,)),
            sems((peers,)),
            sems((peers,)),
        ],
        compiler_params=pltpu.CompilerParams(
            collective_id=0, has_side_effects=True, vmem_limit_bytes=56 * 1024 * 1024
        ),
        cost_estimate=pl.CostEstimate(
            flops=4 * 10**9, bytes_accessed=11 * 10**6, transcendentals=10**6
        ),
    )(
        channel_major(noisy),
        channel_major(target_noise),
        base,
        final_weight.T,
        spatial_project,
        spatial_output,
        temporal_project,
        temporal_output,
    )
    return out.reshape(rows_l, batches, cols).transpose(1, 0, 2)[:, None]


def fits(latents):
    batches, frames_l, rows_l, cols, ch = latents.shape
    per = batches * cols
    return (
        frames_l == 1
        and rows_l == lax.axis_size("frame")
        and rows_l >= 3 * REACH
        and 128 % per == 0
        and (rows_l * per) % 128 == 0
        and ch % 16 == 0
        and 3 * (ch + batches) <= 96
    )


def choose(latents, target_noise, timesteps, *weights):
    plan = fused if fits(latents) else local
    return plan(latents, target_noise, timesteps, *weights)


def solution(mesh):
    data = P("grp", "frame", "row", None, None)
    return jax.shard_map(
        choose,
        mesh=mesh,
        in_specs=(data, data, P("grp")) + (P(),) * 7,
        out_specs=P("grp", "frame", "row", None),
        check_vma=False,
    )
```

```python
import functools
import math

import jax
import jax.numpy as jnp
from jax import lax
from jax.experimental import pallas as pl
from jax.experimental.pallas import tpu as pltpu
from jax.sharding import PartitionSpec as P

HEAD_DIM = 72
HEADS = 8
STEPS = 1000
REACH = 2
HI = lax.Precision.HIGHEST
F32 = jnp.float32
MESH = pl.DeviceIdType.MESH


def noise_levels(timesteps):
    counter = jnp.arange(STEPS, dtype=F32)
    betas_all = 0.0001 + (0.02 - 0.0001) * counter / (STEPS - 1)
    log_keep = jnp.cumsum(jnp.log1p(-betas_all))
    selector = (jnp.arange(STEPS, dtype=jnp.int32)[None, :] == timesteps[:, None]).astype(F32)
    log_bar = jnp.dot(selector, log_keep, precision=HI)
    kept_share = jnp.exp(log_bar)
    return (jnp.sqrt(kept_share), jnp.sqrt(1.0 - kept_share))


def time_embed(timesteps, time_weight):
    halfway = time_weight.shape[0] // 2
    freqs_all = jnp.exp(-math.log(10000.0) * jnp.arange(halfway, dtype=F32) / halfway)
    angles = timesteps.astype(F32)[:, None] * freqs_all[None, :]
    features = jnp.concatenate([jnp.cos(angles), jnp.sin(angles)], axis=-1).astype(jnp.bfloat16)
    return jnp.dot(features, time_weight, preferred_element_type=F32)


def pieces(value, count):
    parts = []
    for _ in range(count):
        part = value.astype(jnp.bfloat16)
        parts.append(part)
        value = value - part.astype(F32)
    return parts


def wide_dot(value, weight, count=2):
    rows = value.shape[0]
    out = jnp.dot(jnp.concatenate(pieces(value, count), axis=0), weight, preferred_element_type=F32)
    return sum(out[i * rows : (i + 1) * rows] for i in range(count))


def centre(value):
    return value - jnp.mean(value, axis=-1, keepdims=True)


def local(
    latents,
    target_noise,
    timesteps,
    patch_weight,
    time_weight,
    spatial_project,
    spatial_output,
    temporal_project,
    temporal_output,
    final_weight,
):
    batches, frames_l, rows_l, cols, ch = latents.shape
    peers, halves = lax.axis_size("frame"), lax.axis_size("row")
    fi, gi = lax.axis_index("frame"), lax.axis_index("row")
    frames, rows = frames_l * peers, rows_l * halves
    places = rows_l * cols // peers
    q_rows, q_cols = max(1, places // cols), min(cols, places)
    width = patch_weight.shape[1]
    inner = spatial_output.shape[0]
    scale = 1.0 / math.sqrt(HEAD_DIM)

    signal, spread = noise_levels(timesteps)
    noisy = (
        signal[:, None, None, None, None] * latents
        + spread[:, None, None, None, None] * target_noise
    ).astype(jnp.bfloat16)
    time_vector = time_embed(timesteps, time_weight)

    whole = lax.all_gather(
        noisy.reshape(batches, frames_l, rows_l, cols * ch), ("frame", "row"), axis=0, tiled=False
    )
    whole = whole.reshape(peers, halves, batches, frames_l, rows_l, cols * ch)
    whole = whole.transpose(2, 0, 3, 1, 4, 5).reshape(batches, frames, rows, cols * ch)
    target = lax.all_to_all(
        target_noise.reshape(batches, frames_l, peers, places * ch),
        "frame",
        split_axis=2,
        concat_axis=1,
        tiled=True,
    ).reshape(batches * frames * places, ch)

    first = gi * rows_l + (fi * places) // cols
    column = (fi * places) % cols
    k_rows = q_rows + 2 * REACH
    padded = jnp.pad(whole, ((0, 0), (0, 0), (REACH, REACH), (0, 0)))
    near = lax.dynamic_slice_in_dim(padded, first, k_rows, axis=2).reshape(
        batches, frames, k_rows, cols, ch
    )
    own = lax.dynamic_slice_in_dim(near[:, :, REACH : REACH + q_rows], column, q_cols, axis=3)

    base = jnp.concatenate([patch_weight.astype(F32), time_vector], axis=0)
    base_c = centre(base)
    feats = base.shape[0]
    spatial = wide_dot(base_c, spatial_project, 3).reshape(feats, 3, HEADS, HEAD_DIM)
    mixer = jnp.einsum("ahe,bhe->hab", spatial[:, 0], spatial[:, 1], precision=HI) * scale
    out_heads = spatial_output.reshape(HEADS, HEAD_DIM, width).astype(F32)
    carried = jnp.einsum("ahe,hed->had", spatial[:, 2], out_heads, precision=HI)
    full_c = jnp.concatenate([base_c, centre(carried).reshape(HEADS * feats, width)], axis=0)
    temporal = wide_dot(full_c, temporal_project, 2)

    def lifted(tokens):
        mark = jnp.broadcast_to(
            jnp.eye(batches, dtype=F32)[:, None, None, None, :], tokens.shape[:-1] + (batches,)
        )
        return jnp.concatenate([tokens.astype(F32), mark], axis=-1)

    def scaled(tokens):
        stream = jnp.einsum("bfrca,ad->bfrcd", tokens, base_c, precision=HI)
        return tokens * lax.rsqrt(jnp.mean(stream * stream, axis=-1, keepdims=True) + 1e-06)

    near_l, own_l = lifted(near), lifted(own)
    keys = scaled(near_l).reshape(batches, frames, k_rows * cols, feats)
    query = scaled(own_l).reshape(batches, frames, places, feats)
    query = jnp.einsum("bfqa,hac->bfhqc", query, mixer, precision=HI)
    scores = jnp.einsum("bfhqc,bfkc->bfhqk", query, keys, precision=HI)
    key_row = jnp.arange(k_rows * cols, dtype=jnp.int32) // cols
    query_row = jnp.arange(places, dtype=jnp.int32) // q_cols
    off = key_row[None, :] - query_row[:, None]
    there = first + key_row - REACH
    inside = ((off >= 0) & (off <= 2 * REACH)) & ((there >= 0) & (there < rows))[None, :]
    scores = jnp.where(inside, scores, -1e30)
    exponent = jnp.exp(scores - jnp.max(scores, axis=-1, keepdims=True))
    weights = exponent / jnp.sum(exponent, axis=-1, keepdims=True)
    mixed = jnp.einsum("bfhqk,bfkc->bfqhc", weights, keys, precision=HI)
    tokens = batches * frames * places
    state = jnp.concatenate(
        [own_l.reshape(tokens, feats), mixed.reshape(tokens, HEADS * feats)], axis=-1
    )

    stream = jnp.dot(state, full_c, precision=HI)
    share = lax.rsqrt(jnp.mean(stream * stream, axis=-1, keepdims=True) + 1e-06)
    projected = (jnp.dot(state, temporal, precision=HI) * share).astype(jnp.bfloat16)
    shaped = projected.reshape(batches, frames, places, 3, HEADS, HEAD_DIM)
    scores = (
        jnp.einsum(
            "bfphe,bgphe->bphfg", shaped[:, :, :, 0], shaped[:, :, :, 1], preferred_element_type=F32
        )
        * scale
    )
    exponent = jnp.exp(scores - jnp.max(scores, axis=-1, keepdims=True))
    weights = (exponent / jnp.sum(exponent, axis=-1, keepdims=True)).astype(jnp.bfloat16)
    mixed = (
        jnp.einsum("bphfg,bgphe->bfphe", weights, shaped[:, :, :, 2], preferred_element_type=F32)
        .astype(jnp.bfloat16)
        .reshape(tokens, inner)
    )
    stream = stream + jnp.dot(mixed, temporal_output, preferred_element_type=F32)
    stream = centre(stream)
    share = lax.rsqrt(jnp.mean(stream * stream, axis=-1, keepdims=True) + 1e-06)
    predicted = jnp.dot(
        (stream * share).astype(jnp.bfloat16), final_weight, preferred_element_type=F32
    )
    gap = predicted - target
    errors = jnp.mean(gap * gap, axis=-1).reshape(batches, frames, places)
    errors = lax.all_to_all(errors, "frame", split_axis=1, concat_axis=2, tiled=True)
    return errors.reshape(batches, frames_l, rows_l, cols)


def dot(a, b, axes=((1,), (0,)), precision=None):
    return lax.dot_general(a, b, (axes, ((), ())), precision=precision, preferred_element_type=F32)


NT = ((1,), (1,))


def fused_kernel(
    peers,
    halves,
    times_ref,
    lat_ref,
    noise_ref,
    patch_ref,
    final_ref,
    tw_hbm,
    sp_hbm,
    so_hbm,
    tp_hbm,
    to_hbm,
    out_ref,
    tw,
    sp,
    so,
    tp,
    to,
    w_sem,
    x_ref,
    target_ref,
    near,
    goal,
    err_out,
    err_in,
    full,
    gt,
    state,
    stream1,
    qkv,
    mixed_t,
    x_send,
    x_recv,
    h_send,
    h_recv,
    t_send,
    t_recv,
    e_send,
    e_recv,
):
    batches, _, rows_l, ch, cols = lat_ref.shape
    lanes = x_ref.shape[-1]
    per = batches * cols
    pair = lanes // per
    width = patch_ref.shape[1]
    inner = so.shape[0]
    feats = ch + 8
    depth = full.shape[0]
    window = 2 * REACH + 1
    fi, gi = lax.axis_index("frame"), lax.axis_index("row")
    pairs = ((tw_hbm, tw), (sp_hbm, sp), (so_hbm, so), (tp_hbm, tp), (to_hbm, to))
    weight_copies = [
        pltpu.make_async_copy(src, dst, w_sem.at[i]) for i, (src, dst) in enumerate(pairs)
    ]
    for copy in weight_copies:
        copy.start()

    barrier = pltpu.get_barrier_semaphore()
    for df in range(peers):
        for dg in range(halves):
            if df or dg:
                pl.semaphore_signal(
                    barrier,
                    inc=1,
                    device_id={
                        "frame": lax.rem(fi + df, peers),
                        "row": lax.rem(gi + dg, halves),
                    },
                    device_id_type=MESH,
                )

    index = 128 * lax.broadcasted_iota(jnp.int32, (8, 128), 0) + lax.broadcasted_iota(
        jnp.int32, (8, 128), 1
    )
    logs = jnp.log1p(-(0.0001 + (0.02 - 0.0001) * index.astype(F32) / (STEPS - 1)))
    logs = jnp.where(index < STEPS, logs, 0.0)
    noisy = []
    for b in range(batches):
        kept = jnp.where(index <= times_ref[b], logs, 0.0)
        kept = jnp.exp(jnp.sum(jnp.sum(kept, axis=1, keepdims=True), axis=0, keepdims=True))
        signal, spread = jnp.sqrt(kept)[None], jnp.sqrt(1.0 - kept)[None]
        noisy.append(signal * lat_ref[b, 0] + spread * noise_ref[b, 0])
    blank = [jnp.zeros((rows_l, ch, lanes - per), F32)] if lanes > per else []
    x_ref[...] = jnp.concatenate(noisy + blank, axis=2).astype(jnp.bfloat16)
    target_ref[...] = jnp.concatenate(
        [noise_ref[b, 0] for b in range(batches)] + blank, axis=2
    )
    pl.semaphore_wait(barrier, peers * halves - 1)

    def start_of(place):
        return jnp.clip(place - REACH, 0, rows_l - window)

    def x_copy(peer):
        return pltpu.make_async_remote_copy(
            src_ref=x_ref.at[pl.ds(start_of(peer), window)],
            dst_ref=near.at[fi, pl.ds(0, window)],
            send_sem=x_send.at[peer],
            recv_sem=x_recv.at[fi],
            device_id={"frame": peer, "row": gi},
            device_id_type=MESH,
        )

    def t_copy(peer):
        return pltpu.make_async_remote_copy(
            src_ref=target_ref.at[peer],
            dst_ref=goal.at[fi],
            send_sem=t_send.at[peer],
            recv_sem=t_recv.at[fi],
            device_id={"frame": peer, "row": gi},
            device_id_type=MESH,
        )

    def halo_copy(slot, peer, half, first):
        return pltpu.make_async_remote_copy(
            src_ref=x_ref.at[pl.ds(first, REACH)],
            dst_ref=near.at[fi, pl.ds(window, REACH)],
            send_sem=h_send.at[slot],
            recv_sem=h_recv.at[fi],
            device_id={"frame": peer, "row": half},
            device_id_type=MESH,
        )

    def halos(action):
        for i in range(REACH):

            @pl.when(gi < halves - 1)
            def _():
                action(halo_copy(i, i, gi + 1, rows_l - REACH))

            @pl.when(gi > 0)
            def _():
                action(halo_copy(REACH + i, peers - REACH + i, gi - 1, 0))

    for k in range(1, peers):
        x_copy(lax.rem(fi + k, peers)).start()
    halos(lambda copy: copy.start())
    for k in range(1, peers):
        t_copy(lax.rem(fi + k, peers)).start()
    near[fi, 0:window] = x_ref[pl.ds(start_of(fi), window)]
    goal[fi] = target_ref[fi]
    takes_halo = ((fi < REACH) & (gi > 0)) | ((fi >= peers - REACH) & (gi < halves - 1))

    @pl.when(jnp.logical_not(takes_halo))
    def _():
        near[:, window:] = jnp.zeros((peers, REACH, ch, lanes), near.dtype)

    halfway = tw.shape[0] // 2
    row = lax.broadcasted_iota(jnp.int32, (8, halfway), 0)
    place = lax.broadcasted_iota(jnp.int32, (8, halfway), 1)
    when = jnp.zeros((8, halfway), jnp.int32)
    for b in range(batches):
        when = jnp.where(row == b, times_ref[b], when)
    angles = when.astype(F32) * jnp.exp(-math.log(10000.0) * place.astype(F32) / halfway)
    used = row < batches
    features = jnp.concatenate(
        [jnp.where(used, jnp.cos(angles), 0.0), jnp.where(used, jnp.sin(angles), 0.0)], axis=1
    ).astype(jnp.bfloat16)
    weight_copies[0].wait()
    base = jnp.concatenate([patch_ref[...].astype(F32), dot(features, tw[...])], axis=0)
    base_c = base - jnp.mean(base, axis=-1, keepdims=True)
    b1, b2, b3 = pieces(base_c, 3)
    weight_copies[1].wait()
    wide = dot(jnp.concatenate([b1, b2, b3], axis=0), sp[...], NT)
    spatial = wide[:feats] + wide[feats : 2 * feats] + wide[2 * feats :]
    sq, sk, sv = (spatial[:, i * inner : (i + 1) * inner] for i in range(3))
    owner = lax.broadcasted_iota(jnp.int32, (feats, inner), 1) // HEAD_DIM

    def by_head(value):
        return jnp.concatenate(
            [jnp.where(owner == h, value, 0.0) for h in range(HEADS)], axis=0
        )

    sk3 = jnp.concatenate([sk] * 3 + [jnp.zeros((128 - 3 * feats, inner), F32)], axis=0)
    mixer = dot(by_head(sq), sk3, NT, HI) * (1.0 / math.sqrt(HEAD_DIM))
    mixer = jnp.concatenate(
        [mixer[h * feats : (h + 1) * feats] for h in range(HEADS)], axis=1
    )
    mixer = jnp.concatenate(pieces(mixer, 3), axis=0)
    v1, v2 = pieces(by_head(sv), 2)
    weight_copies[2].wait()
    carried = dot(v1, so[...]) + dot(v2, so[...])
    carried = carried - jnp.mean(carried, axis=-1, keepdims=True)
    rest = depth - feats * (HEADS + 2)
    full[...] = jnp.concatenate(
        [base_c, carried, base_c - b1.astype(F32), jnp.zeros((rest, width), F32)], axis=0
    ).astype(jnp.bfloat16)
    small = dot(base_c, base_c, NT, HI) * (1.0 / width)
    small = jnp.concatenate(pieces(small, 3), axis=0)
    weight_copies[3].wait()
    gt[...] = dot(tp[...], full[...], NT).astype(jnp.bfloat16)

    for k in range(1, peers):
        other = lax.rem(fi + k, peers)
        x_copy(other).wait_send()
        pltpu.make_async_remote_copy(
            src_ref=x_ref.at[pl.ds(0, window)],
            dst_ref=near.at[other, pl.ds(0, window)],
            send_sem=x_send.at[other],
            recv_sem=x_recv.at[other],
            device_id={"frame": other, "row": gi},
            device_id_type=MESH,
        ).wait_recv()
    halos(lambda copy: copy.wait_send())

    @pl.when(takes_halo)
    def _():
        for k in range(peers):
            pltpu.make_async_remote_copy(
                src_ref=x_ref.at[pl.ds(0, REACH)],
                dst_ref=near.at[k, pl.ds(window, REACH)],
                send_sem=h_send.at[0],
                recv_sem=h_recv.at[k],
                device_id={"frame": k, "row": lax.rem(gi + 1, halves)},
                device_id_type=MESH,
            ).wait_recv()

    span = -(-window * cols // lanes) * lanes
    spots = []
    key_lane = lax.broadcasted_iota(jnp.int32, (1, span), 1)
    bias = jnp.full((1, span), -1e30, F32)
    for d in range(-REACH, REACH + 1):
        lr = fi + d
        spots.append(
            jnp.where(
                lr < 0,
                window + lr + REACH,
                jnp.where(lr >= rows_l, window + lr - rows_l, lr - start_of(fi)),
            )
        )
        there = gi * rows_l + lr
        level = jnp.where((there >= 0) & (there < rows_l * halves), 0.0, -1e30).astype(F32)
        bias = jnp.where(key_lane // cols == d + REACH, level, bias)

    tail = [jnp.zeros((ch, span - window * cols), F32)] if span > window * cols else []
    groups, owns = [], []
    for f in range(peers):
        seen = [near[f, spot].astype(F32) for spot in spots]
        owns.append(seen[REACH][:, :per])
        for b in range(batches):
            groups.append(
                jnp.concatenate([v[:, b * cols : (b + 1) * cols] for v in seen] + tail, axis=1)
            )

    def lifted(value, video):
        mark = (
            video == lax.broadcasted_iota(jnp.int32, (feats - ch, value.shape[1]), 0)
        ).astype(F32)
        return jnp.concatenate([value, mark], axis=0)

    def spread_of(value):
        part = dot(small, value.astype(jnp.bfloat16))
        part = part[:feats] + part[feats : 2 * feats] + part[2 * feats :]
        var = jnp.sum(value * part, axis=0, keepdims=True)
        return lax.rsqrt(jnp.maximum(var, 0.0) + 1e-06)

    own = jnp.concatenate(owns, axis=1)
    tokens = own.shape[1]
    video = lax.broadcasted_iota(jnp.int32, (feats - ch, tokens), 1) % per // cols
    own = lifted(own, video)
    state[0:feats, :] = own
    state[feats * (HEADS + 1) : feats * (HEADS + 2), :] = own
    state[feats * (HEADS + 2) :, :] = jnp.zeros((rest, tokens), F32)
    turned_own = jnp.concatenate(
        [own] * 3 + [jnp.broadcast_to(spread_of(own), (128 - 3 * feats, tokens))], axis=0
    ).T
    ask = dot(turned_own[:, : 3 * feats].astype(jnp.bfloat16), mixer)
    ask = ask * turned_own[:, 3 * feats : 3 * feats + 1]
    lead = ask.astype(jnp.bfloat16).astype(F32)
    lane = lax.broadcasted_iota(jnp.int32, ask.shape, 1) % 128
    ask3 = jnp.where(lane < 2 * feats, lead, ask - lead).astype(jnp.bfloat16)

    key_video = [
        jnp.full((feats - ch, span), b, jnp.int32) for b in range(batches)
    ]
    tiles_of_u = []
    for g, value in enumerate(groups):
        value = lifted(value, key_video[g % batches])
        y = value * spread_of(value)
        high = y.astype(jnp.bfloat16)
        low = y - high.astype(F32)
        high = high.astype(F32)
        keys3 = jnp.concatenate(
            [high, low, high, jnp.zeros((128 - 3 * feats, span), F32)], axis=0
        ).astype(jnp.bfloat16)
        values = jnp.concatenate([high, low, jnp.ones((16, span), F32)], axis=0)
        q3 = jnp.concatenate(
            [
                ask3[g * cols : (g + 1) * cols, h * 128 : (h + 1) * 128]
                for h in range(HEADS)
            ],
            axis=0,
        )
        scores = dot(q3, keys3) + bias
        weight = jnp.exp(scores - jnp.max(scores, axis=1, keepdims=True))
        both = dot(values.astype(jnp.bfloat16), weight.astype(jnp.bfloat16), NT)
        tiles_of_u.append(
            (both[:feats] + both[feats : 2 * feats]) * (1.0 / both[2 * feats : 2 * feats + 1])
        )
    for h in range(HEADS):
        state[feats * (h + 1) : feats * (h + 2), :] = jnp.concatenate(
            [u[:, h * cols : (h + 1) * cols] for u in tiles_of_u], axis=1
        )

    z = state[...]
    stream1[...] = dot(z.T.astype(jnp.bfloat16), full[...])
    square = stream1[...]
    square = (square * square).astype(jnp.bfloat16)
    var = dot(jnp.ones((16, width), jnp.bfloat16), square, NT)[0:1] * (1.0 / width)
    qkv[...] = dot(gt[...], z.astype(jnp.bfloat16)) * lax.rsqrt(var + 1e-06)
    tiles = peers // pair
    scale = 1.0 / math.sqrt(HEAD_DIM)

    def tile_of(part, h, t):
        top = part * inner + h * HEAD_DIM
        return qkv[top : top + HEAD_DIM, t * lanes : (t + 1) * lanes]

    def turned(value, s):
        return pltpu.roll(value, s * per, 1) if s else value

    for h in range(HEADS):
        ks = [turned(tile_of(1, h, t), s) for t in range(tiles) for s in range(pair)]
        vs = [turned(tile_of(2, h, t), s) for t in range(tiles) for s in range(pair)]
        for p in range(tiles):
            q = tile_of(0, h, p) * scale
            logits = [jnp.sum(q * k, axis=0, keepdims=True) for k in ks]
            top = functools.reduce(jnp.maximum, logits)
            exps = [jnp.exp(s - top) for s in logits]
            total = 1.0 / functools.reduce(jnp.add, exps)
            acc = functools.reduce(
                jnp.add, [(e * total) * v for e, v in zip(exps, vs)]
            )
            mixed_t[h * HEAD_DIM : (h + 1) * HEAD_DIM, p * lanes : (p + 1) * lanes] = acc

    weight_copies[4].wait()
    stream = stream1[...] + dot(mixed_t[...].T.astype(jnp.bfloat16), to[...])
    stream = stream - jnp.mean(stream, axis=-1, keepdims=True)
    share = lax.rsqrt(jnp.mean(stream * stream, axis=-1, keepdims=True) + 1e-06)
    predicted = dot(final_ref[...], (stream * share).astype(jnp.bfloat16), NT)

    for k in range(1, peers):
        other = lax.rem(fi + k, peers)
        t_copy(other).wait_send()
        pltpu.make_async_remote_copy(
            src_ref=target_ref.at[0],
            dst_ref=goal.at[other],
            send_sem=t_send.at[other],
            recv_sem=t_recv.at[other],
            device_id={"frame": other, "row": gi},
            device_id_type=MESH,
        ).wait_recv()
    aim = jnp.concatenate([goal[f][:, :per] for f in range(peers)], axis=1)
    gap = predicted - aim
    errors = jnp.mean(gap * gap, axis=0, keepdims=True)
    for t in range(tiles):
        err_out[t] = jnp.broadcast_to(errors[:, t * lanes : (t + 1) * lanes], (8, lanes))

    def e_copy(peer, source, other):
        return pltpu.make_async_remote_copy(
            src_ref=err_out.at[peer // pair],
            dst_ref=err_in.at[source],
            send_sem=e_send.at[peer],
            recv_sem=e_recv.at[source],
            device_id={"frame": other, "row": gi},
            device_id_type=MESH,
        )

    for k in range(1, peers):
        other = lax.rem(fi + k, peers)
        e_copy(other, fi, other).start()
    err_in[fi] = err_out[fi // pair]
    for k in range(1, peers):
        other = lax.rem(fi + k, peers)
        e_copy(other, fi, other).wait_send()
        e_copy(fi, other, other).wait_recv()
    got = jnp.concatenate([err_in[k, 0:1] for k in range(peers)], axis=0)
    result = got[:, :per]
    for s in range(1, pair):
        result = jnp.where(lax.rem(fi, pair) == s, got[:, s * per : (s + 1) * per], result)
    for b in range(batches):
        out_ref[b, 0] = result[:, b * cols : (b + 1) * cols]


def fused(
    latents,
    target_noise,
    timesteps,
    patch_weight,
    time_weight,
    spatial_project,
    spatial_output,
    temporal_project,
    temporal_output,
    final_weight,
):
    batches, frames_l, rows_l, cols, ch = latents.shape
    peers, halves = lax.axis_size("frame"), lax.axis_size("row")
    width, inner = patch_weight.shape[1], spatial_output.shape[0]
    per, lanes = batches * cols, 128
    feats = ch + 8
    tokens = peers * per
    depth = -(-(feats * (HEADS + 2)) // 128) * 128
    bf16 = jnp.bfloat16
    vmem, anywhere = pl.BlockSpec(memory_space=pltpu.VMEM), pl.BlockSpec(memory_space=pl.ANY)
    smem = pl.BlockSpec(memory_space=pltpu.SMEM)
    sems = pltpu.SemaphoreType.DMA
    return pl.pallas_call(
        functools.partial(fused_kernel, peers, halves),
        out_shape=jax.ShapeDtypeStruct((batches, frames_l, rows_l, cols), F32),
        in_specs=[smem] + [vmem] * 4 + [anywhere] * 5,
        out_specs=vmem,
        scratch_shapes=[
            pltpu.VMEM(time_weight.shape, bf16),
            pltpu.VMEM(spatial_project.shape[::-1], bf16),
            pltpu.VMEM(spatial_output.shape, bf16),
            pltpu.VMEM(temporal_project.shape[::-1], bf16),
            pltpu.VMEM(temporal_output.shape, bf16),
            sems((5,)),
            pltpu.VMEM((rows_l, ch, lanes), bf16),
            pltpu.VMEM((rows_l, ch, lanes), F32),
            pltpu.VMEM((peers, 3 * REACH + 1, ch, lanes), bf16),
            pltpu.VMEM((peers, ch, lanes), F32),
            pltpu.VMEM((tokens // lanes, 8, lanes), F32),
            pltpu.VMEM((peers, 8, lanes), F32),
            pltpu.VMEM((depth, width), bf16),
            pltpu.VMEM((3 * inner, depth), bf16),
            pltpu.VMEM((depth, tokens), F32),
            pltpu.VMEM((tokens, width), F32),
            pltpu.VMEM((3 * inner, tokens), F32),
            pltpu.VMEM((inner, tokens), F32),
            sems((peers,)),
            sems((peers,)),
            sems((2 * REACH,)),
            sems((peers,)),
            sems((peers,)),
            sems((peers,)),
            sems((peers,)),
            sems((peers,)),
        ],
        compiler_params=pltpu.CompilerParams(
            collective_id=0, has_side_effects=True, vmem_limit_bytes=56 * 1024 * 1024
        ),
        cost_estimate=pl.CostEstimate(
            flops=4 * 10**9, bytes_accessed=11 * 10**6, transcendentals=10**6
        ),
    )(
        timesteps,
        latents.transpose(0, 1, 2, 4, 3),
        target_noise.transpose(0, 1, 2, 4, 3),
        patch_weight,
        final_weight.T,
        time_weight,
        spatial_project.T,
        spatial_output,
        temporal_project.T,
        temporal_output,
    )


def fits(latents):
    batches, frames_l, rows_l, cols, ch = latents.shape
    per = batches * cols
    return (
        frames_l == 1
        and rows_l == lax.axis_size("frame")
        and rows_l >= 3 * REACH
        and 128 % per == 0
        and (rows_l * per) % 128 == 0
        and ch % 16 == 0
        and batches <= 8
        and 3 * (ch + 8) < 128
    )


def choose(latents, target_noise, timesteps, *weights):
    plan = fused if fits(latents) else local
    return plan(latents, target_noise, timesteps, *weights)


def solution(mesh):
    data = P("grp", "frame", "row", None, None)
    return jax.shard_map(
        choose,
        mesh=mesh,
        in_specs=(data, data, P("grp")) + (P(),) * 7,
        out_specs=P("grp", "frame", "row", None),
        check_vma=False,
    )
```

```python
import functools
import math

import jax
import jax.numpy as jnp
from jax import lax
from jax.experimental import pallas as pl
from jax.experimental.pallas import tpu as pltpu
from jax.sharding import PartitionSpec as P

HEAD_DIM = 72
HEADS = 8
STEPS = 1000
REACH = 2
STAGE = 8
HI = lax.Precision.HIGHEST
F32 = jnp.float32
MESH = pl.DeviceIdType.MESH


def noise_levels(timesteps):
    counter = jnp.arange(STEPS, dtype=F32)
    betas_all = 0.0001 + (0.02 - 0.0001) * counter / (STEPS - 1)
    log_keep = jnp.cumsum(jnp.log1p(-betas_all))
    selector = (jnp.arange(STEPS, dtype=jnp.int32)[None, :] == timesteps[:, None]).astype(F32)
    log_bar = jnp.dot(selector, log_keep, precision=HI)
    kept_share = jnp.exp(log_bar)
    return (jnp.sqrt(kept_share), jnp.sqrt(1.0 - kept_share))


def time_embed(timesteps, time_weight):
    halfway = time_weight.shape[0] // 2
    freqs_all = jnp.exp(-math.log(10000.0) * jnp.arange(halfway, dtype=F32) / halfway)
    angles = timesteps.astype(F32)[:, None] * freqs_all[None, :]
    features = jnp.concatenate([jnp.cos(angles), jnp.sin(angles)], axis=-1).astype(jnp.bfloat16)
    return jnp.dot(features, time_weight, preferred_element_type=F32)


def pieces(value, count):
    parts = []
    for _ in range(count):
        part = value.astype(jnp.bfloat16)
        parts.append(part)
        value = value - part.astype(F32)
    return parts


def wide_dot(value, weight, count=2):
    rows = value.shape[0]
    out = jnp.dot(jnp.concatenate(pieces(value, count), axis=0), weight, preferred_element_type=F32)
    return sum(out[i * rows : (i + 1) * rows] for i in range(count))


def centre(value):
    return value - jnp.mean(value, axis=-1, keepdims=True)


def local(
    latents,
    target_noise,
    timesteps,
    patch_weight,
    time_weight,
    spatial_project,
    spatial_output,
    temporal_project,
    temporal_output,
    final_weight,
):
    batches, frames_l, rows_l, cols, ch = latents.shape
    peers, halves = lax.axis_size("frame"), lax.axis_size("row")
    fi, gi = lax.axis_index("frame"), lax.axis_index("row")
    frames, rows = frames_l * peers, rows_l * halves
    places = rows_l * cols // peers
    q_rows, q_cols = max(1, places // cols), min(cols, places)
    width = patch_weight.shape[1]
    inner = spatial_output.shape[0]
    scale = 1.0 / math.sqrt(HEAD_DIM)

    signal, spread = noise_levels(timesteps)
    noisy = (
        signal[:, None, None, None, None] * latents
        + spread[:, None, None, None, None] * target_noise
    ).astype(jnp.bfloat16)
    time_vector = time_embed(timesteps, time_weight)

    whole = lax.all_gather(
        noisy.reshape(batches, frames_l, rows_l, cols * ch), ("frame", "row"), axis=0, tiled=False
    )
    whole = whole.reshape(peers, halves, batches, frames_l, rows_l, cols * ch)
    whole = whole.transpose(2, 0, 3, 1, 4, 5).reshape(batches, frames, rows, cols * ch)
    target = lax.all_to_all(
        target_noise.reshape(batches, frames_l, peers, places * ch),
        "frame",
        split_axis=2,
        concat_axis=1,
        tiled=True,
    ).reshape(batches * frames * places, ch)

    first = gi * rows_l + (fi * places) // cols
    column = (fi * places) % cols
    k_rows = q_rows + 2 * REACH
    padded = jnp.pad(whole, ((0, 0), (0, 0), (REACH, REACH), (0, 0)))
    near = lax.dynamic_slice_in_dim(padded, first, k_rows, axis=2).reshape(
        batches, frames, k_rows, cols, ch
    )
    own = lax.dynamic_slice_in_dim(near[:, :, REACH : REACH + q_rows], column, q_cols, axis=3)

    base = jnp.concatenate([patch_weight.astype(F32), time_vector], axis=0)
    base_c = centre(base)
    feats = base.shape[0]
    spatial = wide_dot(base_c, spatial_project, 3).reshape(feats, 3, HEADS, HEAD_DIM)
    mixer = jnp.einsum("ahe,bhe->hab", spatial[:, 0], spatial[:, 1], precision=HI) * scale
    out_heads = spatial_output.reshape(HEADS, HEAD_DIM, width).astype(F32)
    carried = jnp.einsum("ahe,hed->had", spatial[:, 2], out_heads, precision=HI)
    full_c = jnp.concatenate([base_c, centre(carried).reshape(HEADS * feats, width)], axis=0)
    temporal = wide_dot(full_c, temporal_project, 2)

    def lifted(tokens):
        mark = jnp.broadcast_to(
            jnp.eye(batches, dtype=F32)[:, None, None, None, :], tokens.shape[:-1] + (batches,)
        )
        return jnp.concatenate([tokens.astype(F32), mark], axis=-1)

    def scaled(tokens):
        stream = jnp.einsum("bfrca,ad->bfrcd", tokens, base_c, precision=HI)
        return tokens * lax.rsqrt(jnp.mean(stream * stream, axis=-1, keepdims=True) + 1e-06)

    near_l, own_l = lifted(near), lifted(own)
    keys = scaled(near_l).reshape(batches, frames, k_rows * cols, feats)
    query = scaled(own_l).reshape(batches, frames, places, feats)
    query = jnp.einsum("bfqa,hac->bfhqc", query, mixer, precision=HI)
    scores = jnp.einsum("bfhqc,bfkc->bfhqk", query, keys, precision=HI)
    key_row = jnp.arange(k_rows * cols, dtype=jnp.int32) // cols
    query_row = jnp.arange(places, dtype=jnp.int32) // q_cols
    off = key_row[None, :] - query_row[:, None]
    there = first + key_row - REACH
    inside = ((off >= 0) & (off <= 2 * REACH)) & ((there >= 0) & (there < rows))[None, :]
    scores = jnp.where(inside, scores, -1e30)
    exponent = jnp.exp(scores - jnp.max(scores, axis=-1, keepdims=True))
    weights = exponent / jnp.sum(exponent, axis=-1, keepdims=True)
    mixed = jnp.einsum("bfhqk,bfkc->bfqhc", weights, keys, precision=HI)
    tokens = batches * frames * places
    state = jnp.concatenate(
        [own_l.reshape(tokens, feats), mixed.reshape(tokens, HEADS * feats)], axis=-1
    )

    stream = jnp.dot(state, full_c, precision=HI)
    share = lax.rsqrt(jnp.mean(stream * stream, axis=-1, keepdims=True) + 1e-06)
    projected = (jnp.dot(state, temporal, precision=HI) * share).astype(jnp.bfloat16)
    shaped = projected.reshape(batches, frames, places, 3, HEADS, HEAD_DIM)
    scores = (
        jnp.einsum(
            "bfphe,bgphe->bphfg", shaped[:, :, :, 0], shaped[:, :, :, 1], preferred_element_type=F32
        )
        * scale
    )
    exponent = jnp.exp(scores - jnp.max(scores, axis=-1, keepdims=True))
    weights = (exponent / jnp.sum(exponent, axis=-1, keepdims=True)).astype(jnp.bfloat16)
    mixed = (
        jnp.einsum("bphfg,bgphe->bfphe", weights, shaped[:, :, :, 2], preferred_element_type=F32)
        .astype(jnp.bfloat16)
        .reshape(tokens, inner)
    )
    stream = stream + jnp.dot(mixed, temporal_output, preferred_element_type=F32)
    stream = centre(stream)
    share = lax.rsqrt(jnp.mean(stream * stream, axis=-1, keepdims=True) + 1e-06)
    predicted = jnp.dot(
        (stream * share).astype(jnp.bfloat16), final_weight, preferred_element_type=F32
    )
    gap = predicted - target
    errors = jnp.mean(gap * gap, axis=-1).reshape(batches, frames, places)
    errors = lax.all_to_all(errors, "frame", split_axis=1, concat_axis=2, tiled=True)
    return errors.reshape(batches, frames_l, rows_l, cols)


def dot(a, b, axes=((1,), (0,)), precision=None):
    return lax.dot_general(a, b, (axes, ((), ())), precision=precision, preferred_element_type=F32)


NT = ((1,), (1,))


def fused_kernel(
    peers,
    halves,
    times_ref,
    lat_ref,
    noise_ref,
    patch_ref,
    final_ref,
    tw_hbm,
    sp_hbm,
    so_hbm,
    tp_hbm,
    to_hbm,
    out_ref,
    tw,
    sp,
    so,
    tp,
    to,
    w_sem,
    x_ref,
    target_ref,
    near,
    goal,
    err_out,
    err_in,
    full,
    gt,
    state,
    stream1,
    qkv,
    mixed_t,
    x_send,
    x_recv,
    h_send,
    h_recv,
    t_send,
    t_recv,
    e_send,
    e_recv,
):
    batches, _, rows_l, ch, cols = lat_ref.shape
    lanes = x_ref.shape[-1]
    per = batches * cols
    pair = lanes // per
    width = patch_ref.shape[1]
    inner = so.shape[0]
    feats = ch + 8
    depth = full.shape[0]
    window = 2 * REACH + 1
    fi, gi = lax.axis_index("frame"), lax.axis_index("row")
    pairs = ((tw_hbm, tw), (sp_hbm, sp), (so_hbm, so), (tp_hbm, tp), (to_hbm, to))
    weight_copies = [
        pltpu.make_async_copy(src, dst, w_sem.at[i]) for i, (src, dst) in enumerate(pairs)
    ]
    for copy in weight_copies:
        copy.start()

    barrier = pltpu.get_barrier_semaphore()
    for df in range(peers):
        for dg in range(halves):
            if df or dg:
                pl.semaphore_signal(
                    barrier,
                    inc=1,
                    device_id={
                        "frame": lax.rem(fi + df, peers),
                        "row": lax.rem(gi + dg, halves),
                    },
                    device_id_type=MESH,
                )

    index = 128 * lax.broadcasted_iota(jnp.int32, (8, 128), 0) + lax.broadcasted_iota(
        jnp.int32, (8, 128), 1
    )
    logs = jnp.log1p(-(0.0001 + (0.02 - 0.0001) * index.astype(F32) / (STEPS - 1)))
    logs = jnp.where(index < STEPS, logs, 0.0)
    noisy = []
    for b in range(batches):
        kept = jnp.where(index <= times_ref[b], logs, 0.0)
        kept = jnp.exp(jnp.sum(jnp.sum(kept, axis=1, keepdims=True), axis=0, keepdims=True))
        signal, spread = jnp.sqrt(kept)[None], jnp.sqrt(1.0 - kept)[None]
        noisy.append(signal * lat_ref[b, 0] + spread * noise_ref[b, 0])
    blank = [jnp.zeros((rows_l, ch, lanes - per), F32)] if lanes > per else []
    x_ref[...] = jnp.concatenate(noisy + blank, axis=2).astype(jnp.bfloat16)
    target_ref[...] = jnp.concatenate(
        [noise_ref[b, 0] for b in range(batches)] + blank, axis=2
    )
    pl.semaphore_wait(barrier, peers * halves - 1)

    def start_of(place):
        return jnp.clip(place - REACH, 0, rows_l - window)

    def x_copy(peer):
        return pltpu.make_async_remote_copy(
            src_ref=x_ref.at[pl.ds(start_of(peer), window)],
            dst_ref=near.at[fi, pl.ds(0, window)],
            send_sem=x_send.at[peer],
            recv_sem=x_recv.at[fi],
            device_id={"frame": peer, "row": gi},
            device_id_type=MESH,
        )

    def t_copy(peer):
        return pltpu.make_async_remote_copy(
            src_ref=target_ref.at[peer],
            dst_ref=goal.at[fi],
            send_sem=t_send.at[peer],
            recv_sem=t_recv.at[fi],
            device_id={"frame": peer, "row": gi},
            device_id_type=MESH,
        )

    def halo_copy(slot, peer, half, first):
        return pltpu.make_async_remote_copy(
            src_ref=x_ref.at[pl.ds(first, REACH)],
            dst_ref=near.at[fi, pl.ds(window, REACH)],
            send_sem=h_send.at[slot],
            recv_sem=h_recv.at[fi],
            device_id={"frame": peer, "row": half},
            device_id_type=MESH,
        )

    def halos(action):
        for i in range(REACH):

            @pl.when(gi < halves - 1)
            def _():
                action(halo_copy(i, i, gi + 1, rows_l - REACH))

            @pl.when(gi > 0)
            def _():
                action(halo_copy(REACH + i, peers - REACH + i, gi - 1, 0))

    for k in range(1, peers):
        x_copy(lax.rem(fi + k, peers)).start()
    halos(lambda copy: copy.start())
    for k in range(1, peers):
        t_copy(lax.rem(fi + k, peers)).start()
    near[fi, 0:window] = x_ref[pl.ds(start_of(fi), window)]
    goal[fi] = target_ref[fi]
    takes_halo = ((fi < REACH) & (gi > 0)) | ((fi >= peers - REACH) & (gi < halves - 1))

    @pl.when(jnp.logical_not(takes_halo))
    def _():
        near[:, window:] = jnp.zeros((peers, REACH, ch, lanes), near.dtype)

    halfway = tw.shape[0] // 2
    row = lax.broadcasted_iota(jnp.int32, (8, halfway), 0)
    place = lax.broadcasted_iota(jnp.int32, (8, halfway), 1)
    when = jnp.zeros((8, halfway), jnp.int32)
    for b in range(batches):
        when = jnp.where(row == b, times_ref[b], when)
    angles = when.astype(F32) * jnp.exp(-math.log(10000.0) * place.astype(F32) / halfway)
    used = row < batches
    features = jnp.concatenate(
        [jnp.where(used, jnp.cos(angles), 0.0), jnp.where(used, jnp.sin(angles), 0.0)], axis=1
    ).astype(jnp.bfloat16)
    weight_copies[0].wait()
    base = jnp.concatenate([patch_ref[...].astype(F32), dot(features, tw[...])], axis=0)
    base_c = base - jnp.mean(base, axis=-1, keepdims=True)
    b1, b2, b3 = pieces(base_c, 3)
    weight_copies[1].wait()
    wide = dot(jnp.concatenate([b1, b2, b3], axis=0), sp[...], NT)
    spatial = wide[:feats] + wide[feats : 2 * feats] + wide[2 * feats :]
    sq, sk, sv = (spatial[:, i * inner : (i + 1) * inner] for i in range(3))
    owner = lax.broadcasted_iota(jnp.int32, (feats, inner), 1) // HEAD_DIM

    def by_head(value):
        return jnp.concatenate(
            [jnp.where(owner == h, value, 0.0) for h in range(HEADS)], axis=0
        )

    sk3 = jnp.concatenate([sk] * 3 + [jnp.zeros((128 - 3 * feats, inner), F32)], axis=0)
    mixer = dot(by_head(sq), sk3, NT, HI) * (1.0 / math.sqrt(HEAD_DIM))
    mixer = jnp.concatenate(
        [mixer[h * feats : (h + 1) * feats] for h in range(HEADS)], axis=1
    )
    mixer = jnp.concatenate(pieces(mixer, 3), axis=0)
    v1, v2 = pieces(by_head(sv), 2)
    weight_copies[2].wait()
    carried = dot(v1, so[...]) + dot(v2, so[...])
    carried = carried - jnp.mean(carried, axis=-1, keepdims=True)
    rest = depth - feats * (HEADS + 2)
    full[...] = jnp.concatenate(
        [base_c, carried, base_c - b1.astype(F32), jnp.zeros((rest, width), F32)], axis=0
    ).astype(jnp.bfloat16)
    small = dot(base_c, base_c, NT, HI) * (1.0 / width)
    small = jnp.concatenate(pieces(small, 3), axis=0)
    weight_copies[3].wait()
    gt[...] = dot(tp[...], full[...], NT).astype(jnp.bfloat16)

    for k in range(1, peers):
        other = lax.rem(fi + k, peers)
        x_copy(other).wait_send()
        pltpu.make_async_remote_copy(
            src_ref=x_ref.at[pl.ds(0, window)],
            dst_ref=near.at[other, pl.ds(0, window)],
            send_sem=x_send.at[other],
            recv_sem=x_recv.at[other],
            device_id={"frame": other, "row": gi},
            device_id_type=MESH,
        ).wait_recv()
    halos(lambda copy: copy.wait_send())

    @pl.when(takes_halo)
    def _():
        for k in range(peers):
            pltpu.make_async_remote_copy(
                src_ref=x_ref.at[pl.ds(0, REACH)],
                dst_ref=near.at[k, pl.ds(window, REACH)],
                send_sem=h_send.at[0],
                recv_sem=h_recv.at[k],
                device_id={"frame": k, "row": lax.rem(gi + 1, halves)},
                device_id_type=MESH,
            ).wait_recv()

    span = -(-window * cols // lanes) * lanes
    spots = []
    key_lane = lax.broadcasted_iota(jnp.int32, (1, span), 1)
    bias = jnp.full((1, span), -1e30, F32)
    for d in range(-REACH, REACH + 1):
        lr = fi + d
        spots.append(
            jnp.where(
                lr < 0,
                window + lr + REACH,
                jnp.where(lr >= rows_l, window + lr - rows_l, lr - start_of(fi)),
            )
        )
        there = gi * rows_l + lr
        level = jnp.where((there >= 0) & (there < rows_l * halves), 0.0, -1e30).astype(F32)
        bias = jnp.where(key_lane // cols == d + REACH, level, bias)

    tail = [jnp.zeros((ch, span - window * cols), F32)] if span > window * cols else []
    groups, owns = [], []
    for f in range(peers):
        seen = [near[f, spot].astype(F32) for spot in spots]
        owns.append(seen[REACH][:, :per])
        for b in range(batches):
            groups.append(
                jnp.concatenate([v[:, b * cols : (b + 1) * cols] for v in seen] + tail, axis=1)
            )

    def lifted(value, video):
        mark = (
            video == lax.broadcasted_iota(jnp.int32, (feats - ch, value.shape[1]), 0)
        ).astype(F32)
        return jnp.concatenate([value, mark], axis=0)

    def spread_of(value):
        part = dot(small, value.astype(jnp.bfloat16))
        part = part[:feats] + part[feats : 2 * feats] + part[2 * feats :]
        var = jnp.sum(value * part, axis=0, keepdims=True)
        return lax.rsqrt(jnp.maximum(var, 0.0) + 1e-06)

    own = jnp.concatenate(owns, axis=1)
    tokens = own.shape[1]
    video = lax.broadcasted_iota(jnp.int32, (feats - ch, tokens), 1) % per // cols
    own = lifted(own, video)
    state[0:feats, :] = own
    state[feats * (HEADS + 1) : feats * (HEADS + 2), :] = own
    state[feats * (HEADS + 2) :, :] = jnp.zeros((rest, tokens), F32)
    turned_own = jnp.concatenate(
        [own] * 3 + [jnp.broadcast_to(spread_of(own), (128 - 3 * feats, tokens))], axis=0
    ).T
    ask = dot(turned_own[:, : 3 * feats].astype(jnp.bfloat16), mixer)
    ask = ask * turned_own[:, 3 * feats : 3 * feats + 1]
    lead = ask.astype(jnp.bfloat16).astype(F32)
    lane = lax.broadcasted_iota(jnp.int32, ask.shape, 1) % 128
    ask3 = jnp.where(lane < 2 * feats, lead, ask - lead)
    ask3 = jnp.where(lane == 3 * feats, 1.0, ask3).astype(jnp.bfloat16)

    count = len(groups)
    near_all = jnp.concatenate(groups, axis=1)
    video = lax.broadcasted_iota(jnp.int32, (feats - ch, count * span), 1) // span % batches
    near_all = lifted(near_all, video)
    y = near_all * spread_of(near_all)
    high = y.astype(jnp.bfloat16).astype(F32)
    low = y - high
    blocked = jnp.concatenate([bias] * count, axis=1)
    keys3 = jnp.concatenate(
        [high, low, high, blocked, jnp.zeros((127 - 3 * feats, count * span), F32)], axis=0
    ).astype(jnp.bfloat16)
    values = jnp.concatenate([high, low, jnp.ones((16, count * span), F32)], axis=0)
    values = values.astype(jnp.bfloat16)
    tiles_of_u = []
    for first in range(0, count, STAGE):
        some = range(first, min(first + STAGE, count))
        scores = [
            dot(
                jnp.concatenate(
                    [
                        ask3[g * cols : (g + 1) * cols, h * 128 : (h + 1) * 128]
                        for h in range(HEADS)
                    ],
                    axis=0,
                ),
                keys3[:, g * span : (g + 1) * span],
            )
            for g in some
        ]
        tops = [jnp.max(v, axis=1, keepdims=True) for v in scores]
        weights = [jnp.exp(v - t).astype(jnp.bfloat16) for v, t in zip(scores, tops)]
        sums = [
            dot(values[:, g * span : (g + 1) * span], w, NT) for g, w in zip(some, weights)
        ]
        tiles_of_u += [
            (v[:feats] + v[feats : 2 * feats]) * (1.0 / v[2 * feats : 2 * feats + 1])
            for v in sums
        ]
    for h in range(HEADS):
        state[feats * (h + 1) : feats * (h + 2), :] = jnp.concatenate(
            [u[:, h * cols : (h + 1) * cols] for u in tiles_of_u], axis=1
        )

    z = state[...]
    stream1[...] = dot(z.T.astype(jnp.bfloat16), full[...])
    square = stream1[...]
    square = (square * square).astype(jnp.bfloat16)
    var = dot(jnp.ones((16, width), jnp.bfloat16), square, NT)[0:1] * (1.0 / width)
    qkv[...] = dot(gt[...], z.astype(jnp.bfloat16)) * lax.rsqrt(var + 1e-06)
    tiles = peers // pair
    scale = 1.0 / math.sqrt(HEAD_DIM)

    def tile_of(part, h, t):
        top = part * inner + h * HEAD_DIM
        return qkv[top : top + HEAD_DIM, t * lanes : (t + 1) * lanes]

    def turned(value, s):
        return pltpu.roll(value, s * per, 1) if s else value

    shifts = [(t, s) for t in range(tiles) for s in range(pair)]
    logits = [[[] for _ in shifts] for _ in range(tiles)]
    for h in range(HEADS):
        ks = [turned(tile_of(1, h, t), s) for t, s in shifts]
        for p in range(tiles):
            q = tile_of(0, h, p) * scale
            for slot, k in zip(logits[p], ks):
                slot.append(jnp.sum(q * k, axis=0, keepdims=True))
    shares = []
    for p in range(tiles):
        rows = [jnp.concatenate(slot, axis=0) for slot in logits[p]]
        top = functools.reduce(jnp.maximum, rows)
        exps = [jnp.exp(v - top) for v in rows]
        total = 1.0 / functools.reduce(jnp.add, exps)
        shares.append([e * total for e in exps])
    for h in range(HEADS):
        vs = [turned(tile_of(2, h, t), s) for t, s in shifts]
        for p in range(tiles):
            mixed_t[h * HEAD_DIM : (h + 1) * HEAD_DIM, p * lanes : (p + 1) * lanes] = (
                functools.reduce(jnp.add, [w[h : h + 1] * v for w, v in zip(shares[p], vs)])
            )

    weight_copies[4].wait()
    stream = stream1[...] + dot(mixed_t[...].T.astype(jnp.bfloat16), to[...])
    stream = stream - jnp.mean(stream, axis=-1, keepdims=True)
    share = lax.rsqrt(jnp.mean(stream * stream, axis=-1, keepdims=True) + 1e-06)
    predicted = dot(final_ref[...], (stream * share).astype(jnp.bfloat16), NT)

    for k in range(1, peers):
        other = lax.rem(fi + k, peers)
        t_copy(other).wait_send()
        pltpu.make_async_remote_copy(
            src_ref=target_ref.at[0],
            dst_ref=goal.at[other],
            send_sem=t_send.at[other],
            recv_sem=t_recv.at[other],
            device_id={"frame": other, "row": gi},
            device_id_type=MESH,
        ).wait_recv()
    aim = jnp.concatenate([goal[f][:, :per] for f in range(peers)], axis=1)
    gap = predicted - aim
    errors = jnp.sum(gap * gap, axis=0, keepdims=True)
    for t in range(tiles):
        err_out[t] = jnp.broadcast_to(errors[:, t * lanes : (t + 1) * lanes], (8, lanes))

    def e_copy(peer, source, other):
        return pltpu.make_async_remote_copy(
            src_ref=err_out.at[peer // pair],
            dst_ref=err_in.at[source],
            send_sem=e_send.at[peer],
            recv_sem=e_recv.at[source],
            device_id={"frame": other, "row": gi},
            device_id_type=MESH,
        )

    for k in range(1, peers):
        other = lax.rem(fi + k, peers)
        e_copy(other, fi, other).start()
    err_in[fi] = err_out[fi // pair]
    for k in range(1, peers):
        other = lax.rem(fi + k, peers)
        e_copy(other, fi, other).wait_send()
        e_copy(fi, other, other).wait_recv()
    got = jnp.concatenate([err_in[k, 0:1] for k in range(peers)], axis=0)
    result = got[:, :per]
    for s in range(1, pair):
        result = jnp.where(lax.rem(fi, pair) == s, got[:, s * per : (s + 1) * per], result)
    for b in range(batches):
        out_ref[b, 0] = result[:, b * cols : (b + 1) * cols]


def fused(
    latents,
    target_noise,
    timesteps,
    patch_weight,
    time_weight,
    spatial_project,
    spatial_output,
    temporal_project,
    temporal_output,
    final_weight,
):
    batches, frames_l, rows_l, cols, ch = latents.shape
    peers, halves = lax.axis_size("frame"), lax.axis_size("row")
    width, inner = patch_weight.shape[1], spatial_output.shape[0]
    per, lanes = batches * cols, 128
    feats = ch + 8
    tokens = peers * per
    depth = -(-(feats * (HEADS + 2)) // 128) * 128
    bf16 = jnp.bfloat16
    vmem, anywhere = pl.BlockSpec(memory_space=pltpu.VMEM), pl.BlockSpec(memory_space=pl.ANY)
    smem = pl.BlockSpec(memory_space=pltpu.SMEM)
    sems = pltpu.SemaphoreType.DMA
    summed = pl.pallas_call(
        functools.partial(fused_kernel, peers, halves),
        out_shape=jax.ShapeDtypeStruct((batches, frames_l, rows_l, cols), F32),
        in_specs=[smem] + [vmem] * 4 + [anywhere] * 5,
        out_specs=vmem,
        scratch_shapes=[
            pltpu.VMEM(time_weight.shape, bf16),
            pltpu.VMEM(spatial_project.shape[::-1], bf16),
            pltpu.VMEM(spatial_output.shape, bf16),
            pltpu.VMEM(temporal_project.shape[::-1], bf16),
            pltpu.VMEM(temporal_output.shape, bf16),
            sems((5,)),
            pltpu.VMEM((rows_l, ch, lanes), bf16),
            pltpu.VMEM((rows_l, ch, lanes), F32),
            pltpu.VMEM((peers, 3 * REACH + 1, ch, lanes), bf16),
            pltpu.VMEM((peers, ch, lanes), F32),
            pltpu.VMEM((tokens // lanes, 8, lanes), F32),
            pltpu.VMEM((peers, 8, lanes), F32),
            pltpu.VMEM((depth, width), bf16),
            pltpu.VMEM((3 * inner, depth), bf16),
            pltpu.VMEM((depth, tokens), F32),
            pltpu.VMEM((tokens, width), F32),
            pltpu.VMEM((3 * inner, tokens), F32),
            pltpu.VMEM((inner, tokens), F32),
            sems((peers,)),
            sems((peers,)),
            sems((2 * REACH,)),
            sems((peers,)),
            sems((peers,)),
            sems((peers,)),
            sems((peers,)),
            sems((peers,)),
        ],
        compiler_params=pltpu.CompilerParams(
            collective_id=0, has_side_effects=True, vmem_limit_bytes=56 * 1024 * 1024
        ),
        cost_estimate=pl.CostEstimate(
            flops=4 * 10**9, bytes_accessed=11 * 10**6, transcendentals=10**6
        ),
    )(
        timesteps,
        latents.transpose(0, 1, 2, 4, 3),
        target_noise.transpose(0, 1, 2, 4, 3),
        patch_weight,
        final_weight.T,
        time_weight,
        spatial_project.T,
        spatial_output,
        temporal_project.T,
        temporal_output,
    )
    return summed * (1.0 / ch)


def fits(latents):
    batches, frames_l, rows_l, cols, ch = latents.shape
    per = batches * cols
    return (
        frames_l == 1
        and rows_l == lax.axis_size("frame")
        and rows_l >= 3 * REACH
        and 128 % per == 0
        and (rows_l * per) % 128 == 0
        and ch % 16 == 0
        and batches <= 8
        and 3 * (ch + 8) < 128
    )


def choose(latents, target_noise, timesteps, *weights):
    plan = fused if fits(latents) else local
    return plan(latents, target_noise, timesteps, *weights)


def solution(mesh):
    data = P("grp", "frame", "row", None, None)
    return jax.shard_map(
        choose,
        mesh=mesh,
        in_specs=(data, data, P("grp")) + (P(),) * 7,
        out_specs=P("grp", "frame", "row", None),
        check_vma=False,
    )
```

```python
import functools
import math

import jax
import jax.numpy as jnp
from jax import lax
from jax.experimental import pallas as pl
from jax.experimental.pallas import tpu as pltpu
from jax.sharding import PartitionSpec as P

HEAD_DIM = 72
HEADS = 8
STEPS = 1000
REACH = 2
STAGE = 16
HI = lax.Precision.HIGHEST
F32 = jnp.float32
MESH = pl.DeviceIdType.MESH


def noise_levels(timesteps):
    counter = jnp.arange(STEPS, dtype=F32)
    betas_all = 0.0001 + (0.02 - 0.0001) * counter / (STEPS - 1)
    log_keep = jnp.cumsum(jnp.log1p(-betas_all))
    selector = (jnp.arange(STEPS, dtype=jnp.int32)[None, :] == timesteps[:, None]).astype(F32)
    log_bar = jnp.dot(selector, log_keep, precision=HI)
    kept_share = jnp.exp(log_bar)
    return (jnp.sqrt(kept_share), jnp.sqrt(1.0 - kept_share))


def time_embed(timesteps, time_weight):
    halfway = time_weight.shape[0] // 2
    freqs_all = jnp.exp(-math.log(10000.0) * jnp.arange(halfway, dtype=F32) / halfway)
    angles = timesteps.astype(F32)[:, None] * freqs_all[None, :]
    features = jnp.concatenate([jnp.cos(angles), jnp.sin(angles)], axis=-1).astype(jnp.bfloat16)
    return jnp.dot(features, time_weight, preferred_element_type=F32)


def pieces(value, count):
    parts = []
    for _ in range(count):
        part = value.astype(jnp.bfloat16)
        parts.append(part)
        value = value - part.astype(F32)
    return parts


def wide_dot(value, weight, count=2):
    rows = value.shape[0]
    out = jnp.dot(jnp.concatenate(pieces(value, count), axis=0), weight, preferred_element_type=F32)
    return sum(out[i * rows : (i + 1) * rows] for i in range(count))


def centre(value):
    return value - jnp.mean(value, axis=-1, keepdims=True)


def local(
    latents,
    target_noise,
    timesteps,
    patch_weight,
    time_weight,
    spatial_project,
    spatial_output,
    temporal_project,
    temporal_output,
    final_weight,
):
    batches, frames_l, rows_l, cols, ch = latents.shape
    peers, halves = lax.axis_size("frame"), lax.axis_size("row")
    fi, gi = lax.axis_index("frame"), lax.axis_index("row")
    frames, rows = frames_l * peers, rows_l * halves
    places = rows_l * cols // peers
    q_rows, q_cols = max(1, places // cols), min(cols, places)
    width = patch_weight.shape[1]
    inner = spatial_output.shape[0]
    scale = 1.0 / math.sqrt(HEAD_DIM)

    signal, spread = noise_levels(timesteps)
    noisy = (
        signal[:, None, None, None, None] * latents
        + spread[:, None, None, None, None] * target_noise
    ).astype(jnp.bfloat16)
    time_vector = time_embed(timesteps, time_weight)

    whole = lax.all_gather(
        noisy.reshape(batches, frames_l, rows_l, cols * ch), ("frame", "row"), axis=0, tiled=False
    )
    whole = whole.reshape(peers, halves, batches, frames_l, rows_l, cols * ch)
    whole = whole.transpose(2, 0, 3, 1, 4, 5).reshape(batches, frames, rows, cols * ch)
    target = lax.all_to_all(
        target_noise.reshape(batches, frames_l, peers, places * ch),
        "frame",
        split_axis=2,
        concat_axis=1,
        tiled=True,
    ).reshape(batches * frames * places, ch)

    first = gi * rows_l + (fi * places) // cols
    column = (fi * places) % cols
    k_rows = q_rows + 2 * REACH
    padded = jnp.pad(whole, ((0, 0), (0, 0), (REACH, REACH), (0, 0)))
    near = lax.dynamic_slice_in_dim(padded, first, k_rows, axis=2).reshape(
        batches, frames, k_rows, cols, ch
    )
    own = lax.dynamic_slice_in_dim(near[:, :, REACH : REACH + q_rows], column, q_cols, axis=3)

    base = jnp.concatenate([patch_weight.astype(F32), time_vector], axis=0)
    base_c = centre(base)
    feats = base.shape[0]
    spatial = wide_dot(base_c, spatial_project, 3).reshape(feats, 3, HEADS, HEAD_DIM)
    mixer = jnp.einsum("ahe,bhe->hab", spatial[:, 0], spatial[:, 1], precision=HI) * scale
    out_heads = spatial_output.reshape(HEADS, HEAD_DIM, width).astype(F32)
    carried = jnp.einsum("ahe,hed->had", spatial[:, 2], out_heads, precision=HI)
    full_c = jnp.concatenate([base_c, centre(carried).reshape(HEADS * feats, width)], axis=0)
    temporal = wide_dot(full_c, temporal_project, 2)

    def lifted(tokens):
        mark = jnp.broadcast_to(
            jnp.eye(batches, dtype=F32)[:, None, None, None, :], tokens.shape[:-1] + (batches,)
        )
        return jnp.concatenate([tokens.astype(F32), mark], axis=-1)

    def scaled(tokens):
        stream = jnp.einsum("bfrca,ad->bfrcd", tokens, base_c, precision=HI)
        return tokens * lax.rsqrt(jnp.mean(stream * stream, axis=-1, keepdims=True) + 1e-06)

    near_l, own_l = lifted(near), lifted(own)
    keys = scaled(near_l).reshape(batches, frames, k_rows * cols, feats)
    query = scaled(own_l).reshape(batches, frames, places, feats)
    query = jnp.einsum("bfqa,hac->bfhqc", query, mixer, precision=HI)
    scores = jnp.einsum("bfhqc,bfkc->bfhqk", query, keys, precision=HI)
    key_row = jnp.arange(k_rows * cols, dtype=jnp.int32) // cols
    query_row = jnp.arange(places, dtype=jnp.int32) // q_cols
    off = key_row[None, :] - query_row[:, None]
    there = first + key_row - REACH
    inside = ((off >= 0) & (off <= 2 * REACH)) & ((there >= 0) & (there < rows))[None, :]
    scores = jnp.where(inside, scores, -1e30)
    exponent = jnp.exp(scores - jnp.max(scores, axis=-1, keepdims=True))
    weights = exponent / jnp.sum(exponent, axis=-1, keepdims=True)
    mixed = jnp.einsum("bfhqk,bfkc->bfqhc", weights, keys, precision=HI)
    tokens = batches * frames * places
    state = jnp.concatenate(
        [own_l.reshape(tokens, feats), mixed.reshape(tokens, HEADS * feats)], axis=-1
    )

    stream = jnp.dot(state, full_c, precision=HI)
    share = lax.rsqrt(jnp.mean(stream * stream, axis=-1, keepdims=True) + 1e-06)
    projected = (jnp.dot(state, temporal, precision=HI) * share).astype(jnp.bfloat16)
    shaped = projected.reshape(batches, frames, places, 3, HEADS, HEAD_DIM)
    scores = (
        jnp.einsum(
            "bfphe,bgphe->bphfg", shaped[:, :, :, 0], shaped[:, :, :, 1], preferred_element_type=F32
        )
        * scale
    )
    exponent = jnp.exp(scores - jnp.max(scores, axis=-1, keepdims=True))
    weights = (exponent / jnp.sum(exponent, axis=-1, keepdims=True)).astype(jnp.bfloat16)
    mixed = (
        jnp.einsum("bphfg,bgphe->bfphe", weights, shaped[:, :, :, 2], preferred_element_type=F32)
        .astype(jnp.bfloat16)
        .reshape(tokens, inner)
    )
    stream = stream + jnp.dot(mixed, temporal_output, preferred_element_type=F32)
    stream = centre(stream)
    share = lax.rsqrt(jnp.mean(stream * stream, axis=-1, keepdims=True) + 1e-06)
    predicted = jnp.dot(
        (stream * share).astype(jnp.bfloat16), final_weight, preferred_element_type=F32
    )
    gap = predicted - target
    errors = jnp.mean(gap * gap, axis=-1).reshape(batches, frames, places)
    errors = lax.all_to_all(errors, "frame", split_axis=1, concat_axis=2, tiled=True)
    return errors.reshape(batches, frames_l, rows_l, cols)


def dot(a, b, axes=((1,), (0,)), precision=None):
    return lax.dot_general(a, b, (axes, ((), ())), precision=precision, preferred_element_type=F32)


NT = ((1,), (1,))


def fused_kernel(
    peers,
    halves,
    times_ref,
    lat_ref,
    noise_ref,
    patch_ref,
    final_ref,
    tw_hbm,
    sp_hbm,
    so_hbm,
    tp_hbm,
    to_hbm,
    out_ref,
    tw,
    sp,
    so,
    tp,
    to,
    w_sem,
    x_ref,
    target_ref,
    near,
    goal,
    err_out,
    err_in,
    full,
    gt,
    state,
    stream1,
    qkv,
    mixed_t,
    x_send,
    x_recv,
    h_send,
    h_recv,
    t_send,
    t_recv,
    e_send,
    e_recv,
):
    batches, _, rows_l, ch, cols = lat_ref.shape
    lanes = x_ref.shape[-1]
    per = batches * cols
    pair = lanes // per
    width = patch_ref.shape[1]
    inner = so.shape[0]
    feats = ch + 8
    depth = full.shape[0]
    rest = depth - feats * (HEADS + 2)
    window = 2 * REACH + 1
    fi, gi = lax.axis_index("frame"), lax.axis_index("row")
    pairs = ((tw_hbm, tw), (sp_hbm, sp), (so_hbm, so), (tp_hbm, tp), (to_hbm, to))
    weight_copies = [
        pltpu.make_async_copy(src, dst, w_sem.at[i]) for i, (src, dst) in enumerate(pairs)
    ]
    for copy in weight_copies[:2]:
        copy.start()

    barrier = pltpu.get_barrier_semaphore()
    for df in range(peers):
        for dg in range(halves):
            if df or dg:
                pl.semaphore_signal(
                    barrier,
                    inc=1,
                    device_id={
                        "frame": lax.rem(fi + df, peers),
                        "row": lax.rem(gi + dg, halves),
                    },
                    device_id_type=MESH,
                )

    index = 128 * lax.broadcasted_iota(jnp.int32, (8, 128), 0) + lax.broadcasted_iota(
        jnp.int32, (8, 128), 1
    )
    logs = jnp.log1p(-(0.0001 + (0.02 - 0.0001) * index.astype(F32) / (STEPS - 1)))
    logs = jnp.where(index < STEPS, logs, 0.0)
    noisy = []
    for b in range(batches):
        kept = jnp.where(index <= times_ref[b], logs, 0.0)
        kept = jnp.exp(jnp.sum(jnp.sum(kept, axis=1, keepdims=True), axis=0, keepdims=True))
        signal, spread = jnp.sqrt(kept)[None], jnp.sqrt(1.0 - kept)[None]
        noisy.append(signal * lat_ref[b, 0] + spread * noise_ref[b, 0])
    blank = [jnp.zeros((rows_l, ch, lanes - per), F32)] if lanes > per else []
    x_ref[...] = jnp.concatenate(noisy + blank, axis=2).astype(jnp.bfloat16)
    target_ref[...] = jnp.concatenate(
        [noise_ref[b, 0] for b in range(batches)] + blank, axis=2
    )
    pl.semaphore_wait(barrier, peers * halves - 1)

    def start_of(place):
        return jnp.clip(place - REACH, 0, rows_l - window)

    def x_copy(peer):
        return pltpu.make_async_remote_copy(
            src_ref=x_ref.at[pl.ds(start_of(peer), window)],
            dst_ref=near.at[fi, pl.ds(0, window)],
            send_sem=x_send.at[peer],
            recv_sem=x_recv.at[fi],
            device_id={"frame": peer, "row": gi},
            device_id_type=MESH,
        )

    def t_copy(peer):
        return pltpu.make_async_remote_copy(
            src_ref=target_ref.at[peer],
            dst_ref=goal.at[fi],
            send_sem=t_send.at[peer],
            recv_sem=t_recv.at[fi],
            device_id={"frame": peer, "row": gi},
            device_id_type=MESH,
        )

    def halo_copy(slot, peer, half, first):
        return pltpu.make_async_remote_copy(
            src_ref=x_ref.at[pl.ds(first, REACH)],
            dst_ref=near.at[fi, pl.ds(window, REACH)],
            send_sem=h_send.at[slot],
            recv_sem=h_recv.at[fi],
            device_id={"frame": peer, "row": half},
            device_id_type=MESH,
        )

    def halos(action):
        for i in range(REACH):

            @pl.when(gi < halves - 1)
            def _():
                action(halo_copy(i, i, gi + 1, rows_l - REACH))

            @pl.when(gi > 0)
            def _():
                action(halo_copy(REACH + i, peers - REACH + i, gi - 1, 0))

    for k in range(1, peers):
        x_copy(lax.rem(fi + k, peers)).start()
    halos(lambda copy: copy.start())
    for k in range(1, peers):
        t_copy(lax.rem(fi + k, peers)).start()
    near[fi, 0:window] = x_ref[pl.ds(start_of(fi), window)]
    goal[fi] = target_ref[fi]
    takes_halo = ((fi < REACH) & (gi > 0)) | ((fi >= peers - REACH) & (gi < halves - 1))

    @pl.when(jnp.logical_not(takes_halo))
    def _():
        near[:, window:] = jnp.zeros((peers, REACH, ch, lanes), near.dtype)

    halfway = tw.shape[0] // 2
    row = lax.broadcasted_iota(jnp.int32, (8, halfway), 0)
    place = lax.broadcasted_iota(jnp.int32, (8, halfway), 1)
    when = jnp.zeros((8, halfway), jnp.int32)
    for b in range(batches):
        when = jnp.where(row == b, times_ref[b], when)
    angles = when.astype(F32) * jnp.exp(-math.log(10000.0) * place.astype(F32) / halfway)
    used = row < batches
    features = jnp.concatenate(
        [jnp.where(used, jnp.cos(angles), 0.0), jnp.where(used, jnp.sin(angles), 0.0)], axis=1
    ).astype(jnp.bfloat16)
    weight_copies[0].wait()
    base = jnp.concatenate([patch_ref[...].astype(F32), dot(features, tw[...])], axis=0)
    base_c = base - jnp.mean(base, axis=-1, keepdims=True)
    b1, b2, b3 = pieces(base_c, 3)
    weight_copies[1].wait()
    for copy in weight_copies[2:]:
        copy.start()
    wide = dot(jnp.concatenate([b1, b2, b3], axis=0), sp[...], NT)
    spatial = wide[:feats] + wide[feats : 2 * feats] + wide[2 * feats :]
    sq, sk, sv = (spatial[:, i * inner : (i + 1) * inner] for i in range(3))
    owner = lax.broadcasted_iota(jnp.int32, (feats, inner), 1) // HEAD_DIM

    def by_head(value):
        return jnp.concatenate(
            [jnp.where(owner == h, value, 0.0) for h in range(HEADS)], axis=0
        )

    sk3 = jnp.concatenate([sk] * 3 + [jnp.zeros((128 - 3 * feats, inner), F32)], axis=0)
    mixer = dot(by_head(sq), sk3, NT, HI) * (1.0 / math.sqrt(HEAD_DIM))
    mixer = jnp.concatenate(
        [mixer[h * feats : (h + 1) * feats] for h in range(HEADS)], axis=1
    )
    mixer = jnp.concatenate(pieces(mixer, 3), axis=0)
    small = dot(base_c, base_c, NT, HI) * (1.0 / width)
    small = jnp.concatenate(pieces(small, 3), axis=0)

    for k in range(1, peers):
        other = lax.rem(fi + k, peers)
        x_copy(other).wait_send()
        pltpu.make_async_remote_copy(
            src_ref=x_ref.at[pl.ds(0, window)],
            dst_ref=near.at[other, pl.ds(0, window)],
            send_sem=x_send.at[other],
            recv_sem=x_recv.at[other],
            device_id={"frame": other, "row": gi},
            device_id_type=MESH,
        ).wait_recv()
    halos(lambda copy: copy.wait_send())

    @pl.when(takes_halo)
    def _():
        for k in range(peers):
            pltpu.make_async_remote_copy(
                src_ref=x_ref.at[pl.ds(0, REACH)],
                dst_ref=near.at[k, pl.ds(window, REACH)],
                send_sem=h_send.at[0],
                recv_sem=h_recv.at[k],
                device_id={"frame": k, "row": lax.rem(gi + 1, halves)},
                device_id_type=MESH,
            ).wait_recv()

    weight_copies[2].wait()
    weight_copies[3].wait()
    weight_copies[4].wait()

    span = -(-window * cols // lanes) * lanes
    spots = []
    key_lane = lax.broadcasted_iota(jnp.int32, (1, span), 1)
    bias = jnp.full((1, span), -1e30, F32)
    for d in range(-REACH, REACH + 1):
        lr = fi + d
        spots.append(
            jnp.where(
                lr < 0,
                window + lr + REACH,
                jnp.where(lr >= rows_l, window + lr - rows_l, lr - start_of(fi)),
            )
        )
        there = gi * rows_l + lr
        level = jnp.where((there >= 0) & (there < rows_l * halves), 0.0, -1e30).astype(F32)
        bias = jnp.where(key_lane // cols == d + REACH, level, bias)

    tail = [jnp.zeros((ch, span - window * cols), F32)] if span > window * cols else []
    groups, owns = [], []
    for f in range(peers):
        seen = [near[f, spot].astype(F32) for spot in spots]
        owns.append(seen[REACH][:, :per])
        for b in range(batches):
            groups.append(
                jnp.concatenate([v[:, b * cols : (b + 1) * cols] for v in seen] + tail, axis=1)
            )

    def lifted(value, video):
        mark = (
            video == lax.broadcasted_iota(jnp.int32, (feats - ch, value.shape[1]), 0)
        ).astype(F32)
        return jnp.concatenate([value, mark], axis=0)

    def spread_of(value):
        part = dot(small, value.astype(jnp.bfloat16))
        part = part[:feats] + part[feats : 2 * feats] + part[2 * feats :]
        var = jnp.sum(value * part, axis=0, keepdims=True)
        return lax.rsqrt(jnp.maximum(var, 0.0) + 1e-06)

    own = jnp.concatenate(owns, axis=1)
    tokens = own.shape[1]
    video = lax.broadcasted_iota(jnp.int32, (feats - ch, tokens), 1) % per // cols
    own = lifted(own, video)
    state[0:feats, :] = own
    state[feats * (HEADS + 1) : feats * (HEADS + 2), :] = own
    state[feats * (HEADS + 2) :, :] = jnp.zeros((rest, tokens), F32)
    turned_own = jnp.concatenate(
        [own] * 3 + [jnp.broadcast_to(spread_of(own), (128 - 3 * feats, tokens))], axis=0
    ).T
    ask = dot(turned_own[:, : 3 * feats].astype(jnp.bfloat16), mixer)
    ask = ask * turned_own[:, 3 * feats : 3 * feats + 1]
    lead = ask.astype(jnp.bfloat16).astype(F32)
    lane = lax.broadcasted_iota(jnp.int32, ask.shape, 1) % 128
    ask3 = jnp.where(lane < 2 * feats, lead, ask - lead)
    ask3 = jnp.where(lane == 3 * feats, 1.0, ask3).astype(jnp.bfloat16)

    v1, v2 = pieces(by_head(sv), 2)
    carried = dot(v1, so[...]) + dot(v2, so[...])
    carried = carried - jnp.mean(carried, axis=-1, keepdims=True)
    full[...] = jnp.concatenate(
        [base_c, carried, base_c - b1.astype(F32), jnp.zeros((rest, width), F32)], axis=0
    ).astype(jnp.bfloat16)
    gt[...] = dot(tp[...], full[...], NT).astype(jnp.bfloat16)
    count = len(groups)
    near_all = jnp.concatenate(groups, axis=1)
    video = lax.broadcasted_iota(jnp.int32, (feats - ch, count * span), 1) // span % batches
    near_all = lifted(near_all, video)
    y = near_all * spread_of(near_all)
    high = y.astype(jnp.bfloat16).astype(F32)
    low = y - high
    blocked = jnp.concatenate([bias] * count, axis=1)
    keys3 = jnp.concatenate(
        [high, low, high, blocked, jnp.zeros((127 - 3 * feats, count * span), F32)], axis=0
    ).astype(jnp.bfloat16)
    values = jnp.concatenate([high, low, jnp.ones((16, count * span), F32)], axis=0)
    values = values.astype(jnp.bfloat16)
    tiles_of_u = []
    for first in range(0, count, STAGE):
        some = range(first, min(first + STAGE, count))
        scores = [
            dot(
                jnp.concatenate(
                    [
                        ask3[g * cols : (g + 1) * cols, h * 128 : (h + 1) * 128]
                        for h in range(HEADS)
                    ],
                    axis=0,
                ),
                keys3[:, g * span : (g + 1) * span],
            )
            for g in some
        ]
        tops = [jnp.max(v, axis=1, keepdims=True) for v in scores]
        weights = [jnp.exp(v - t).astype(jnp.bfloat16) for v, t in zip(scores, tops)]
        sums = [
            dot(values[:, g * span : (g + 1) * span], w, NT) for g, w in zip(some, weights)
        ]
        tiles_of_u += [
            (v[:feats] + v[feats : 2 * feats]) * (1.0 / v[2 * feats : 2 * feats + 1])
            for v in sums
        ]
    for h in range(HEADS):
        state[feats * (h + 1) : feats * (h + 2), :] = jnp.concatenate(
            [u[:, h * cols : (h + 1) * cols] for u in tiles_of_u], axis=1
        )

    z = state[...]
    stream1[...] = dot(z.T.astype(jnp.bfloat16), full[...])
    square = stream1[...]
    square = (square * square).astype(jnp.bfloat16)
    var = dot(jnp.ones((16, width), jnp.bfloat16), square, NT)[0:1] * (1.0 / width)
    qkv[...] = dot(gt[...], z.astype(jnp.bfloat16)) * lax.rsqrt(var + 1e-06)
    tiles = peers // pair
    scale = 1.0 / math.sqrt(HEAD_DIM)

    def tile_of(part, h, t):
        top = part * inner + h * HEAD_DIM
        return qkv[top : top + HEAD_DIM, t * lanes : (t + 1) * lanes]

    def turned(value, s):
        return pltpu.roll(value, s * per, 1) if s else value

    shifts = [(t, s) for t in range(tiles) for s in range(pair)]
    logits = [[[] for _ in shifts] for _ in range(tiles)]
    for h in range(HEADS):
        ks = [turned(tile_of(1, h, t), s) for t, s in shifts]
        for p in range(tiles):
            q = tile_of(0, h, p) * scale
            for slot, k in zip(logits[p], ks):
                slot.append(jnp.sum(q * k, axis=0, keepdims=True))
    shares = []
    for p in range(tiles):
        rows = [jnp.concatenate(slot, axis=0) for slot in logits[p]]
        top = functools.reduce(jnp.maximum, rows)
        exps = [jnp.exp(v - top) for v in rows]
        total = 1.0 / functools.reduce(jnp.add, exps)
        shares.append([e * total for e in exps])
    for h in range(HEADS):
        vs = [turned(tile_of(2, h, t), s) for t, s in shifts]
        for p in range(tiles):
            mixed_t[h * HEAD_DIM : (h + 1) * HEAD_DIM, p * lanes : (p + 1) * lanes] = (
                functools.reduce(jnp.add, [w[h : h + 1] * v for w, v in zip(shares[p], vs)])
            )

    stream = stream1[...] + dot(mixed_t[...].T.astype(jnp.bfloat16), to[...])
    stream = stream - jnp.mean(stream, axis=-1, keepdims=True)
    share = lax.rsqrt(jnp.mean(stream * stream, axis=-1, keepdims=True) + 1e-06)
    predicted = dot(final_ref[...], (stream * share).astype(jnp.bfloat16), NT)

    for k in range(1, peers):
        other = lax.rem(fi + k, peers)
        t_copy(other).wait_send()
        pltpu.make_async_remote_copy(
            src_ref=target_ref.at[0],
            dst_ref=goal.at[other],
            send_sem=t_send.at[other],
            recv_sem=t_recv.at[other],
            device_id={"frame": other, "row": gi},
            device_id_type=MESH,
        ).wait_recv()
    aim = jnp.concatenate([goal[f][:, :per] for f in range(peers)], axis=1)
    gap = predicted - aim
    errors = jnp.sum(gap * gap, axis=0, keepdims=True)
    for t in range(tiles):
        err_out[t] = jnp.broadcast_to(errors[:, t * lanes : (t + 1) * lanes], (8, lanes))

    def e_copy(peer, source, other):
        return pltpu.make_async_remote_copy(
            src_ref=err_out.at[peer // pair],
            dst_ref=err_in.at[source],
            send_sem=e_send.at[peer],
            recv_sem=e_recv.at[source],
            device_id={"frame": other, "row": gi},
            device_id_type=MESH,
        )

    for k in range(1, peers):
        other = lax.rem(fi + k, peers)
        e_copy(other, fi, other).start()
    err_in[fi] = err_out[fi // pair]
    for k in range(1, peers):
        other = lax.rem(fi + k, peers)
        e_copy(other, fi, other).wait_send()
        e_copy(fi, other, other).wait_recv()
    got = jnp.concatenate([err_in[k, 0:1] for k in range(peers)], axis=0)
    result = got[:, :per]
    for s in range(1, pair):
        result = jnp.where(lax.rem(fi, pair) == s, got[:, s * per : (s + 1) * per], result)
    for b in range(batches):
        out_ref[b, 0] = result[:, b * cols : (b + 1) * cols]


def fused(
    latents,
    target_noise,
    timesteps,
    patch_weight,
    time_weight,
    spatial_project,
    spatial_output,
    temporal_project,
    temporal_output,
    final_weight,
):
    batches, frames_l, rows_l, cols, ch = latents.shape
    peers, halves = lax.axis_size("frame"), lax.axis_size("row")
    width, inner = patch_weight.shape[1], spatial_output.shape[0]
    per, lanes = batches * cols, 128
    feats = ch + 8
    tokens = peers * per
    depth = -(-(feats * (HEADS + 2)) // 128) * 128
    bf16 = jnp.bfloat16
    vmem, anywhere = pl.BlockSpec(memory_space=pltpu.VMEM), pl.BlockSpec(memory_space=pl.ANY)
    smem = pl.BlockSpec(memory_space=pltpu.SMEM)
    sems = pltpu.SemaphoreType.DMA
    summed = pl.pallas_call(
        functools.partial(fused_kernel, peers, halves),
        out_shape=jax.ShapeDtypeStruct((batches, frames_l, rows_l, cols), F32),
        in_specs=[smem] + [vmem] * 4 + [anywhere] * 5,
        out_specs=vmem,
        scratch_shapes=[
            pltpu.VMEM(time_weight.shape, bf16),
            pltpu.VMEM(spatial_project.shape[::-1], bf16),
            pltpu.VMEM(spatial_output.shape, bf16),
            pltpu.VMEM(temporal_project.shape[::-1], bf16),
            pltpu.VMEM(temporal_output.shape, bf16),
            sems((5,)),
            pltpu.VMEM((rows_l, ch, lanes), bf16),
            pltpu.VMEM((rows_l, ch, lanes), F32),
            pltpu.VMEM((peers, 3 * REACH + 1, ch, lanes), bf16),
            pltpu.VMEM((peers, ch, lanes), F32),
            pltpu.VMEM((tokens // lanes, 8, lanes), F32),
            pltpu.VMEM((peers, 8, lanes), F32),
            pltpu.VMEM((depth, width), bf16),
            pltpu.VMEM((3 * inner, depth), bf16),
            pltpu.VMEM((depth, tokens), F32),
            pltpu.VMEM((tokens, width), F32),
            pltpu.VMEM((3 * inner, tokens), F32),
            pltpu.VMEM((inner, tokens), F32),
            sems((peers,)),
            sems((peers,)),
            sems((2 * REACH,)),
            sems((peers,)),
            sems((peers,)),
            sems((peers,)),
            sems((peers,)),
            sems((peers,)),
        ],
        compiler_params=pltpu.CompilerParams(
            collective_id=0, has_side_effects=True, vmem_limit_bytes=56 * 1024 * 1024
        ),
        cost_estimate=pl.CostEstimate(
            flops=4 * 10**9, bytes_accessed=11 * 10**6, transcendentals=10**6
        ),
    )(
        timesteps,
        latents.transpose(0, 1, 2, 4, 3),
        target_noise.transpose(0, 1, 2, 4, 3),
        patch_weight,
        final_weight.T,
        time_weight,
        spatial_project.T,
        spatial_output,
        temporal_project.T,
        temporal_output,
    )
    return summed * (1.0 / ch)


def fits(latents):
    batches, frames_l, rows_l, cols, ch = latents.shape
    per = batches * cols
    return (
        frames_l == 1
        and rows_l == lax.axis_size("frame")
        and rows_l >= 3 * REACH
        and 128 % per == 0
        and (rows_l * per) % 128 == 0
        and ch % 16 == 0
        and batches <= 8
        and 3 * (ch + 8) < 128
    )


def choose(latents, target_noise, timesteps, *weights):
    plan = fused if fits(latents) else local
    return plan(latents, target_noise, timesteps, *weights)


def solution(mesh):
    data = P("grp", "frame", "row", None, None)
    return jax.shard_map(
        choose,
        mesh=mesh,
        in_specs=(data, data, P("grp")) + (P(),) * 7,
        out_specs=P("grp", "frame", "row", None),
        check_vma=False,
    )
```

```python
import functools
import math

import jax
import jax.numpy as jnp
from jax import lax
from jax.experimental import pallas as pl
from jax.experimental.pallas import tpu as pltpu
from jax.sharding import PartitionSpec as P

HEAD_DIM = 72
HEADS = 8
STEPS = 1000
REACH = 2
STAGE = 8
HI = lax.Precision.HIGHEST
F32 = jnp.float32
MESH = pl.DeviceIdType.MESH


def noise_levels(timesteps):
    counter = jnp.arange(STEPS, dtype=F32)
    betas_all = 0.0001 + (0.02 - 0.0001) * counter / (STEPS - 1)
    log_keep = jnp.cumsum(jnp.log1p(-betas_all))
    selector = (jnp.arange(STEPS, dtype=jnp.int32)[None, :] == timesteps[:, None]).astype(F32)
    log_bar = jnp.dot(selector, log_keep, precision=HI)
    kept_share = jnp.exp(log_bar)
    return (jnp.sqrt(kept_share), jnp.sqrt(1.0 - kept_share))


def time_embed(timesteps, time_weight):
    halfway = time_weight.shape[0] // 2
    freqs_all = jnp.exp(-math.log(10000.0) * jnp.arange(halfway, dtype=F32) / halfway)
    angles = timesteps.astype(F32)[:, None] * freqs_all[None, :]
    features = jnp.concatenate([jnp.cos(angles), jnp.sin(angles)], axis=-1).astype(jnp.bfloat16)
    return jnp.dot(features, time_weight, preferred_element_type=F32)


def pieces(value, count):
    parts = []
    for _ in range(count):
        part = value.astype(jnp.bfloat16)
        parts.append(part)
        value = value - part.astype(F32)
    return parts


def wide_dot(value, weight, count=2):
    rows = value.shape[0]
    out = jnp.dot(jnp.concatenate(pieces(value, count), axis=0), weight, preferred_element_type=F32)
    return sum(out[i * rows : (i + 1) * rows] for i in range(count))


def centre(value):
    return value - jnp.mean(value, axis=-1, keepdims=True)


def local(
    latents,
    target_noise,
    timesteps,
    patch_weight,
    time_weight,
    spatial_project,
    spatial_output,
    temporal_project,
    temporal_output,
    final_weight,
):
    batches, frames_l, rows_l, cols, ch = latents.shape
    peers, halves = lax.axis_size("frame"), lax.axis_size("row")
    fi, gi = lax.axis_index("frame"), lax.axis_index("row")
    frames, rows = frames_l * peers, rows_l * halves
    places = rows_l * cols // peers
    q_rows, q_cols = max(1, places // cols), min(cols, places)
    width = patch_weight.shape[1]
    inner = spatial_output.shape[0]
    scale = 1.0 / math.sqrt(HEAD_DIM)

    signal, spread = noise_levels(timesteps)
    noisy = (
        signal[:, None, None, None, None] * latents
        + spread[:, None, None, None, None] * target_noise
    ).astype(jnp.bfloat16)
    time_vector = time_embed(timesteps, time_weight)

    whole = lax.all_gather(
        noisy.reshape(batches, frames_l, rows_l, cols * ch), ("frame", "row"), axis=0, tiled=False
    )
    whole = whole.reshape(peers, halves, batches, frames_l, rows_l, cols * ch)
    whole = whole.transpose(2, 0, 3, 1, 4, 5).reshape(batches, frames, rows, cols * ch)
    target = lax.all_to_all(
        target_noise.reshape(batches, frames_l, peers, places * ch),
        "frame",
        split_axis=2,
        concat_axis=1,
        tiled=True,
    ).reshape(batches * frames * places, ch)

    first = gi * rows_l + (fi * places) // cols
    column = (fi * places) % cols
    k_rows = q_rows + 2 * REACH
    padded = jnp.pad(whole, ((0, 0), (0, 0), (REACH, REACH), (0, 0)))
    near = lax.dynamic_slice_in_dim(padded, first, k_rows, axis=2).reshape(
        batches, frames, k_rows, cols, ch
    )
    own = lax.dynamic_slice_in_dim(near[:, :, REACH : REACH + q_rows], column, q_cols, axis=3)

    base = jnp.concatenate([patch_weight.astype(F32), time_vector], axis=0)
    base_c = centre(base)
    feats = base.shape[0]
    spatial = wide_dot(base_c, spatial_project, 3).reshape(feats, 3, HEADS, HEAD_DIM)
    mixer = jnp.einsum("ahe,bhe->hab", spatial[:, 0], spatial[:, 1], precision=HI) * scale
    out_heads = spatial_output.reshape(HEADS, HEAD_DIM, width).astype(F32)
    carried = jnp.einsum("ahe,hed->had", spatial[:, 2], out_heads, precision=HI)
    full_c = jnp.concatenate([base_c, centre(carried).reshape(HEADS * feats, width)], axis=0)
    temporal = wide_dot(full_c, temporal_project, 2)

    def lifted(tokens):
        mark = jnp.broadcast_to(
            jnp.eye(batches, dtype=F32)[:, None, None, None, :], tokens.shape[:-1] + (batches,)
        )
        return jnp.concatenate([tokens.astype(F32), mark], axis=-1)

    def scaled(tokens):
        stream = jnp.einsum("bfrca,ad->bfrcd", tokens, base_c, precision=HI)
        return tokens * lax.rsqrt(jnp.mean(stream * stream, axis=-1, keepdims=True) + 1e-06)

    near_l, own_l = lifted(near), lifted(own)
    keys = scaled(near_l).reshape(batches, frames, k_rows * cols, feats)
    query = scaled(own_l).reshape(batches, frames, places, feats)
    query = jnp.einsum("bfqa,hac->bfhqc", query, mixer, precision=HI)
    scores = jnp.einsum("bfhqc,bfkc->bfhqk", query, keys, precision=HI)
    key_row = jnp.arange(k_rows * cols, dtype=jnp.int32) // cols
    query_row = jnp.arange(places, dtype=jnp.int32) // q_cols
    off = key_row[None, :] - query_row[:, None]
    there = first + key_row - REACH
    inside = ((off >= 0) & (off <= 2 * REACH)) & ((there >= 0) & (there < rows))[None, :]
    scores = jnp.where(inside, scores, -1e30)
    exponent = jnp.exp(scores - jnp.max(scores, axis=-1, keepdims=True))
    weights = exponent / jnp.sum(exponent, axis=-1, keepdims=True)
    mixed = jnp.einsum("bfhqk,bfkc->bfqhc", weights, keys, precision=HI)
    tokens = batches * frames * places
    state = jnp.concatenate(
        [own_l.reshape(tokens, feats), mixed.reshape(tokens, HEADS * feats)], axis=-1
    )

    stream = jnp.dot(state, full_c, precision=HI)
    share = lax.rsqrt(jnp.mean(stream * stream, axis=-1, keepdims=True) + 1e-06)
    projected = (jnp.dot(state, temporal, precision=HI) * share).astype(jnp.bfloat16)
    shaped = projected.reshape(batches, frames, places, 3, HEADS, HEAD_DIM)
    scores = (
        jnp.einsum(
            "bfphe,bgphe->bphfg", shaped[:, :, :, 0], shaped[:, :, :, 1], preferred_element_type=F32
        )
        * scale
    )
    exponent = jnp.exp(scores - jnp.max(scores, axis=-1, keepdims=True))
    weights = (exponent / jnp.sum(exponent, axis=-1, keepdims=True)).astype(jnp.bfloat16)
    mixed = (
        jnp.einsum("bphfg,bgphe->bfphe", weights, shaped[:, :, :, 2], preferred_element_type=F32)
        .astype(jnp.bfloat16)
        .reshape(tokens, inner)
    )
    stream = stream + jnp.dot(mixed, temporal_output, preferred_element_type=F32)
    stream = centre(stream)
    share = lax.rsqrt(jnp.mean(stream * stream, axis=-1, keepdims=True) + 1e-06)
    predicted = jnp.dot(
        (stream * share).astype(jnp.bfloat16), final_weight, preferred_element_type=F32
    )
    gap = predicted - target
    errors = jnp.mean(gap * gap, axis=-1).reshape(batches, frames, places)
    errors = lax.all_to_all(errors, "frame", split_axis=1, concat_axis=2, tiled=True)
    return errors.reshape(batches, frames_l, rows_l, cols)


def dot(a, b, axes=((1,), (0,)), precision=None):
    return lax.dot_general(a, b, (axes, ((), ())), precision=precision, preferred_element_type=F32)


NT = ((1,), (1,))


def fused_kernel(
    peers,
    halves,
    times_ref,
    lat_ref,
    noise_ref,
    patch_ref,
    final_ref,
    tw_hbm,
    sp_hbm,
    so_hbm,
    tp_hbm,
    to_hbm,
    out_ref,
    tw,
    sp,
    so,
    tp,
    to,
    w_sem,
    x_ref,
    target_ref,
    near,
    goal,
    err_out,
    err_in,
    full,
    gt,
    state,
    stream1,
    qkv,
    mixed_t,
    x_send,
    x_recv,
    h_send,
    h_recv,
    t_send,
    t_recv,
    e_send,
    e_recv,
):
    batches, _, rows_l, ch, cols = lat_ref.shape
    lanes = x_ref.shape[-1]
    per = batches * cols
    pair = lanes // per
    width = patch_ref.shape[1]
    inner = so.shape[0]
    feats = ch + 8
    depth = full.shape[0]
    window = 2 * REACH + 1
    fi, gi = lax.axis_index("frame"), lax.axis_index("row")
    pairs = ((tw_hbm, tw), (sp_hbm, sp), (so_hbm, so), (tp_hbm, tp), (to_hbm, to))
    weight_copies = [
        pltpu.make_async_copy(src, dst, w_sem.at[i]) for i, (src, dst) in enumerate(pairs)
    ]
    for copy in weight_copies:
        copy.start()

    barrier = pltpu.get_barrier_semaphore()
    for df in range(peers):
        for dg in range(halves):
            if df or dg:
                pl.semaphore_signal(
                    barrier,
                    inc=1,
                    device_id={
                        "frame": lax.rem(fi + df, peers),
                        "row": lax.rem(gi + dg, halves),
                    },
                    device_id_type=MESH,
                )

    index = 128 * lax.broadcasted_iota(jnp.int32, (8, 128), 0) + lax.broadcasted_iota(
        jnp.int32, (8, 128), 1
    )
    logs = jnp.log1p(-(0.0001 + (0.02 - 0.0001) * index.astype(F32) / (STEPS - 1)))
    logs = jnp.where(index < STEPS, logs, 0.0)
    noisy = []
    for b in range(batches):
        kept = jnp.where(index <= times_ref[b], logs, 0.0)
        kept = jnp.exp(jnp.sum(jnp.sum(kept, axis=1, keepdims=True), axis=0, keepdims=True))
        signal, spread = jnp.sqrt(kept)[None], jnp.sqrt(1.0 - kept)[None]
        noisy.append(signal * lat_ref[b, 0] + spread * noise_ref[b, 0])
    blank = [jnp.zeros((rows_l, ch, lanes - per), F32)] if lanes > per else []
    rows = jnp.concatenate(noisy, axis=2)
    packed = window // 2 + 1
    empty = jnp.zeros((1, ch, per), F32)
    ahead = jnp.concatenate([rows[packed:], empty], axis=0)
    x_ref[0 : rows_l - packed + 1] = jnp.concatenate(
        [rows[: rows_l - packed + 1], ahead], axis=2
    ).astype(jnp.bfloat16)
    edges = ((rows_l - REACH, rows_l - REACH + 1), (0, 1))
    for i, (one, two) in enumerate(edges):
        x_ref[rows_l - packed + 1 + i] = jnp.concatenate(
            [rows[one], rows[two]], axis=1
        ).astype(jnp.bfloat16)
    target_ref[...] = jnp.concatenate(
        [noise_ref[b, 0] for b in range(batches)] + blank, axis=2
    )
    pl.semaphore_wait(barrier, peers * halves - 1)

    def start_of(place):
        return jnp.clip(place - REACH, 0, rows_l - window)

    def x_copy(peer):
        return pltpu.make_async_remote_copy(
            src_ref=x_ref.at[pl.ds(start_of(peer), packed)],
            dst_ref=near.at[fi, pl.ds(0, packed)],
            send_sem=x_send.at[peer],
            recv_sem=x_recv.at[fi],
            device_id={"frame": peer, "row": gi},
            device_id_type=MESH,
        )

    def t_copy(peer):
        return pltpu.make_async_remote_copy(
            src_ref=target_ref.at[peer],
            dst_ref=goal.at[fi],
            send_sem=t_send.at[peer],
            recv_sem=t_recv.at[fi],
            device_id={"frame": peer, "row": gi},
            device_id_type=MESH,
        )

    def halo_copy(slot, peer, half, first):
        return pltpu.make_async_remote_copy(
            src_ref=x_ref.at[first],
            dst_ref=near.at[fi, packed],
            send_sem=h_send.at[slot],
            recv_sem=h_recv.at[fi],
            device_id={"frame": peer, "row": half},
            device_id_type=MESH,
        )

    def halos(action):
        for i in range(REACH):

            @pl.when(gi < halves - 1)
            def _():
                action(halo_copy(i, i, gi + 1, rows_l - packed + 1))

            @pl.when(gi > 0)
            def _():
                action(halo_copy(REACH + i, peers - REACH + i, gi - 1, rows_l - packed + 2))

    for k in range(1, peers):
        x_copy(lax.rem(fi + k, peers)).start()
    halos(lambda copy: copy.start())
    for k in range(1, peers):
        t_copy(lax.rem(fi + k, peers)).start()
    near[fi, 0:packed] = x_ref[pl.ds(start_of(fi), packed)]
    goal[fi] = target_ref[fi]
    takes_halo = ((fi < REACH) & (gi > 0)) | ((fi >= peers - REACH) & (gi < halves - 1))

    @pl.when(jnp.logical_not(takes_halo))
    def _():
        near[:, packed:] = jnp.zeros((peers, 1, ch, lanes), near.dtype)

    halfway = tw.shape[0] // 2
    row = lax.broadcasted_iota(jnp.int32, (8, halfway), 0)
    place = lax.broadcasted_iota(jnp.int32, (8, halfway), 1)
    when = jnp.zeros((8, halfway), jnp.int32)
    for b in range(batches):
        when = jnp.where(row == b, times_ref[b], when)
    angles = when.astype(F32) * jnp.exp(-math.log(10000.0) * place.astype(F32) / halfway)
    used = row < batches
    features = jnp.concatenate(
        [jnp.where(used, jnp.cos(angles), 0.0), jnp.where(used, jnp.sin(angles), 0.0)], axis=1
    ).astype(jnp.bfloat16)
    weight_copies[0].wait()
    base = jnp.concatenate([patch_ref[...].astype(F32), dot(features, tw[...])], axis=0)
    base_c = base - jnp.mean(base, axis=-1, keepdims=True)
    b1, b2, b3 = pieces(base_c, 3)
    weight_copies[1].wait()
    wide = dot(jnp.concatenate([b1, b2, b3], axis=0), sp[...], NT)
    spatial = wide[:feats] + wide[feats : 2 * feats] + wide[2 * feats :]
    sq, sk, sv = (spatial[:, i * inner : (i + 1) * inner] for i in range(3))
    owner = lax.broadcasted_iota(jnp.int32, (feats, inner), 1) // HEAD_DIM

    def by_head(value):
        return jnp.concatenate(
            [jnp.where(owner == h, value, 0.0) for h in range(HEADS)], axis=0
        )

    sk3 = jnp.concatenate([sk] * 3 + [jnp.zeros((128 - 3 * feats, inner), F32)], axis=0)
    mixer = dot(by_head(sq), sk3, NT, HI) * (1.0 / math.sqrt(HEAD_DIM))
    mixer = jnp.concatenate(
        [mixer[h * feats : (h + 1) * feats] for h in range(HEADS)], axis=1
    )
    mixer = jnp.concatenate(pieces(mixer, 3), axis=0)
    v1, v2 = pieces(by_head(sv), 2)
    weight_copies[2].wait()
    carried = dot(v1, so[...]) + dot(v2, so[...])
    carried = carried - jnp.mean(carried, axis=-1, keepdims=True)
    rest = depth - feats * (HEADS + 2)
    full[...] = jnp.concatenate(
        [base_c, carried, base_c - b1.astype(F32), jnp.zeros((rest, width), F32)], axis=0
    ).astype(jnp.bfloat16)
    small = dot(base_c, base_c, NT, HI) * (1.0 / width)
    small = jnp.concatenate(pieces(small, 3), axis=0)
    weight_copies[3].wait()
    turned_full = dot(tp[...], full[...], NT)
    scale = 1.0 / math.sqrt(HEAD_DIM)
    gt[0:inner] = (turned_full[:inner] * scale).astype(jnp.bfloat16)
    gt[inner:] = turned_full[inner:].astype(jnp.bfloat16)

    for k in range(1, peers):
        other = lax.rem(fi + k, peers)
        x_copy(other).wait_send()
        pltpu.make_async_remote_copy(
            src_ref=x_ref.at[pl.ds(0, packed)],
            dst_ref=near.at[other, pl.ds(0, packed)],
            send_sem=x_send.at[other],
            recv_sem=x_recv.at[other],
            device_id={"frame": other, "row": gi},
            device_id_type=MESH,
        ).wait_recv()
    halos(lambda copy: copy.wait_send())

    @pl.when(takes_halo)
    def _():
        for k in range(peers):
            pltpu.make_async_remote_copy(
                src_ref=x_ref.at[0],
                dst_ref=near.at[k, packed],
                send_sem=h_send.at[0],
                recv_sem=h_recv.at[k],
                device_id={"frame": k, "row": lax.rem(gi + 1, halves)},
                device_id_type=MESH,
            ).wait_recv()

    span = -(-window * cols // lanes) * lanes
    spots = []
    key_lane = lax.broadcasted_iota(jnp.int32, (1, span), 1)
    bias = jnp.full((1, span), -1e30, F32)
    for d in range(-REACH, REACH + 1):
        lr = fi + d
        outside = (lr < 0) | (lr >= rows_l)
        step = jnp.where(lr < 0, lr + REACH, jnp.where(lr >= rows_l, lr - rows_l, lr - start_of(fi)))
        second = jnp.where(outside, step == 1, step >= packed)
        entry = jnp.where(outside, packed, jnp.where(step >= packed, step - packed, step))
        spots.append((entry, second))
        there = gi * rows_l + lr
        level = jnp.where((there >= 0) & (there < rows_l * halves), 0.0, -1e30).astype(F32)
        bias = jnp.where(key_lane // cols == d + REACH, level, bias)

    tail = [jnp.zeros((ch, span - window * cols), F32)] if span > window * cols else []
    groups, owns = [], []
    for f in range(peers):
        seen = [near[f, entry].astype(F32) for entry, _ in spots]
        seen = [
            jnp.where(second, v[:, per:], v[:, :per]) for v, (_, second) in zip(seen, spots)
        ]
        owns.append(seen[REACH])
        for b in range(batches):
            groups.append(
                jnp.concatenate([v[:, b * cols : (b + 1) * cols] for v in seen] + tail, axis=1)
            )

    def lifted(value, video):
        mark = (
            video == lax.broadcasted_iota(jnp.int32, (feats - ch, value.shape[1]), 0)
        ).astype(F32)
        return jnp.concatenate([value, mark], axis=0)

    def spread_of(value):
        part = dot(small, value.astype(jnp.bfloat16))
        part = part[:feats] + part[feats : 2 * feats] + part[2 * feats :]
        var = jnp.sum(value * part, axis=0, keepdims=True)
        return lax.rsqrt(jnp.maximum(var, 0.0) + 1e-06)

    own = jnp.concatenate(owns, axis=1)
    tokens = own.shape[1]
    video = lax.broadcasted_iota(jnp.int32, (feats - ch, tokens), 1) % per // cols
    own = lifted(own, video)
    state[0:feats, :] = own
    state[feats * (HEADS + 1) : feats * (HEADS + 2), :] = own
    state[feats * (HEADS + 2) :, :] = jnp.zeros((rest, tokens), F32)
    turned_own = jnp.concatenate(
        [own] * 3 + [jnp.broadcast_to(spread_of(own), (128 - 3 * feats, tokens))], axis=0
    ).T
    ask = dot(turned_own[:, : 3 * feats].astype(jnp.bfloat16), mixer)
    ask = ask * turned_own[:, 3 * feats : 3 * feats + 1]
    lead = ask.astype(jnp.bfloat16).astype(F32)
    lane = lax.broadcasted_iota(jnp.int32, ask.shape, 1) % 128
    ask3 = jnp.where(lane < 2 * feats, lead, ask - lead)
    ask3 = jnp.where(lane == 3 * feats, 1.0, ask3).astype(jnp.bfloat16)

    count = len(groups)
    near_all = jnp.concatenate(groups, axis=1)
    video = lax.broadcasted_iota(jnp.int32, (feats - ch, count * span), 1) // span % batches
    near_all = lifted(near_all, video)
    y = near_all * spread_of(near_all)
    high = y.astype(jnp.bfloat16).astype(F32)
    low = y - high
    blocked = jnp.concatenate([bias] * count, axis=1)
    keys3 = jnp.concatenate(
        [high, low, high, blocked, jnp.zeros((127 - 3 * feats, count * span), F32)], axis=0
    ).astype(jnp.bfloat16)
    values = jnp.concatenate([high, low, jnp.ones((16, count * span), F32)], axis=0)
    values = values.astype(jnp.bfloat16)
    tiles_of_u = []
    for first in range(0, count, STAGE):
        some = range(first, min(first + STAGE, count))
        scores = [
            dot(
                jnp.concatenate(
                    [
                        ask3[g * cols : (g + 1) * cols, h * 128 : (h + 1) * 128]
                        for h in range(HEADS)
                    ],
                    axis=0,
                ),
                keys3[:, g * span : (g + 1) * span],
            )
            for g in some
        ]
        tops = [jnp.max(v, axis=1, keepdims=True) for v in scores]
        weights = [jnp.exp(v - t).astype(jnp.bfloat16) for v, t in zip(scores, tops)]
        sums = [
            dot(values[:, g * span : (g + 1) * span], w, NT) for g, w in zip(some, weights)
        ]
        tiles_of_u += [
            (v[:feats] + v[feats : 2 * feats]) * (1.0 / v[2 * feats : 2 * feats + 1])
            for v in sums
        ]
    for h in range(HEADS):
        state[feats * (h + 1) : feats * (h + 2), :] = jnp.concatenate(
            [u[:, h * cols : (h + 1) * cols] for u in tiles_of_u], axis=1
        )

    z = state[...]
    stream1[...] = dot(z.T.astype(jnp.bfloat16), full[...])
    square = stream1[...]
    square = (square * square).astype(jnp.bfloat16)
    var = dot(jnp.ones((16, width), jnp.bfloat16), square, NT)[0:1] * (1.0 / width)
    qkv[...] = dot(gt[...], z.astype(jnp.bfloat16)) * lax.rsqrt(var + 1e-06)
    tiles = peers // pair

    def tile_of(part, h, t):
        top = part * inner + h * HEAD_DIM
        return qkv[top : top + HEAD_DIM, t * lanes : (t + 1) * lanes]

    def turned(value, s):
        return pltpu.roll(value, s * per, 1) if s else value

    shifts = [(t, s) for t in range(tiles) for s in range(pair)]
    logits = [[[] for _ in shifts] for _ in range(tiles)]
    for h in range(HEADS):
        ks = [turned(tile_of(1, h, t), s) for t, s in shifts]
        for p in range(tiles):
            q = tile_of(0, h, p)
            for slot, k in zip(logits[p], ks):
                slot.append(jnp.sum(q * k, axis=0, keepdims=True))
    shares = []
    for p in range(tiles):
        rows = [jnp.concatenate(slot, axis=0) for slot in logits[p]]
        top = functools.reduce(jnp.maximum, rows)
        exps = [jnp.exp(v - top) for v in rows]
        total = 1.0 / functools.reduce(jnp.add, exps)
        shares.append([e * total for e in exps])
    for h in range(HEADS):
        vs = [turned(tile_of(2, h, t), s) for t, s in shifts]
        for p in range(tiles):
            mixed_t[h * HEAD_DIM : (h + 1) * HEAD_DIM, p * lanes : (p + 1) * lanes] = (
                functools.reduce(jnp.add, [w[h : h + 1] * v for w, v in zip(shares[p], vs)])
            )

    weight_copies[4].wait()
    stream = stream1[...] + dot(mixed_t[...].astype(jnp.bfloat16).T, to[...])
    stream = stream - jnp.mean(stream, axis=-1, keepdims=True)
    share = lax.rsqrt(jnp.mean(stream * stream, axis=-1, keepdims=True) + 1e-06)
    predicted = dot(final_ref[...], (stream * share).astype(jnp.bfloat16), NT)

    for k in range(1, peers):
        other = lax.rem(fi + k, peers)
        t_copy(other).wait_send()
        pltpu.make_async_remote_copy(
            src_ref=target_ref.at[0],
            dst_ref=goal.at[other],
            send_sem=t_send.at[other],
            recv_sem=t_recv.at[other],
            device_id={"frame": other, "row": gi},
            device_id_type=MESH,
        ).wait_recv()
    aim = jnp.concatenate([goal[f][:, :per] for f in range(peers)], axis=1)
    gap = predicted - aim
    errors = jnp.sum(gap * gap, axis=0, keepdims=True)
    for t in range(tiles):
        err_out[t] = jnp.broadcast_to(errors[:, t * lanes : (t + 1) * lanes], (8, lanes))

    def e_copy(peer, source, other):
        return pltpu.make_async_remote_copy(
            src_ref=err_out.at[peer // pair],
            dst_ref=err_in.at[source],
            send_sem=e_send.at[peer],
            recv_sem=e_recv.at[source],
            device_id={"frame": other, "row": gi},
            device_id_type=MESH,
        )

    for k in range(1, peers):
        other = lax.rem(fi + k, peers)
        e_copy(other, fi, other).start()
    err_in[fi] = err_out[fi // pair]
    for k in range(1, peers):
        other = lax.rem(fi + k, peers)
        e_copy(other, fi, other).wait_send()
        e_copy(fi, other, other).wait_recv()
    got = jnp.concatenate([err_in[k, 0:1] for k in range(peers)], axis=0)
    result = got[:, :per]
    for s in range(1, pair):
        result = jnp.where(lax.rem(fi, pair) == s, got[:, s * per : (s + 1) * per], result)
    for b in range(batches):
        out_ref[b, 0] = result[:, b * cols : (b + 1) * cols]


def fused(
    latents,
    target_noise,
    timesteps,
    patch_weight,
    time_weight,
    spatial_project,
    spatial_output,
    temporal_project,
    temporal_output,
    final_weight,
):
    batches, frames_l, rows_l, cols, ch = latents.shape
    peers, halves = lax.axis_size("frame"), lax.axis_size("row")
    width, inner = patch_weight.shape[1], spatial_output.shape[0]
    per, lanes = batches * cols, 128
    feats = ch + 8
    tokens = peers * per
    depth = -(-(feats * (HEADS + 2)) // 128) * 128
    bf16 = jnp.bfloat16
    vmem, anywhere = pl.BlockSpec(memory_space=pltpu.VMEM), pl.BlockSpec(memory_space=pl.ANY)
    smem = pl.BlockSpec(memory_space=pltpu.SMEM)
    sems = pltpu.SemaphoreType.DMA
    summed = pl.pallas_call(
        functools.partial(fused_kernel, peers, halves),
        out_shape=jax.ShapeDtypeStruct((batches, frames_l, rows_l, cols), F32),
        in_specs=[smem] + [vmem] * 4 + [anywhere] * 5,
        out_specs=vmem,
        scratch_shapes=[
            pltpu.VMEM(time_weight.shape, bf16),
            pltpu.VMEM(spatial_project.shape[::-1], bf16),
            pltpu.VMEM(spatial_output.shape, bf16),
            pltpu.VMEM(temporal_project.shape[::-1], bf16),
            pltpu.VMEM(temporal_output.shape, bf16),
            sems((5,)),
            pltpu.VMEM((rows_l, ch, lanes), bf16),
            pltpu.VMEM((rows_l, ch, lanes), F32),
            pltpu.VMEM((peers, REACH + 2, ch, lanes), bf16),
            pltpu.VMEM((peers, ch, lanes), F32),
            pltpu.VMEM((tokens // lanes, 8, lanes), F32),
            pltpu.VMEM((peers, 8, lanes), F32),
            pltpu.VMEM((depth, width), bf16),
            pltpu.VMEM((3 * inner, depth), bf16),
            pltpu.VMEM((depth, tokens), F32),
            pltpu.VMEM((tokens, width), F32),
            pltpu.VMEM((3 * inner, tokens), F32),
            pltpu.VMEM((inner, tokens), F32),
            sems((peers,)),
            sems((peers,)),
            sems((2 * REACH,)),
            sems((peers,)),
            sems((peers,)),
            sems((peers,)),
            sems((peers,)),
            sems((peers,)),
        ],
        compiler_params=pltpu.CompilerParams(
            collective_id=0, has_side_effects=True, vmem_limit_bytes=56 * 1024 * 1024
        ),
        cost_estimate=pl.CostEstimate(
            flops=4 * 10**9, bytes_accessed=11 * 10**6, transcendentals=10**6
        ),
    )(
        timesteps,
        latents.transpose(0, 1, 2, 4, 3),
        target_noise.transpose(0, 1, 2, 4, 3),
        patch_weight,
        final_weight.T,
        time_weight,
        spatial_project.T,
        spatial_output,
        temporal_project.T,
        temporal_output,
    )
    return summed * (1.0 / ch)


def fits(latents):
    batches, frames_l, rows_l, cols, ch = latents.shape
    per = batches * cols
    return (
        frames_l == 1
        and rows_l == lax.axis_size("frame")
        and rows_l >= 3 * REACH
        and 2 * per == 128
        and REACH == 2
        and (rows_l * per) % 128 == 0
        and ch % 16 == 0
        and batches <= 8
        and 3 * (ch + 8) < 128
    )


def choose(latents, target_noise, timesteps, *weights):
    plan = fused if fits(latents) else local
    return plan(latents, target_noise, timesteps, *weights)


def solution(mesh):
    data = P("grp", "frame", "row", None, None)
    return jax.shard_map(
        choose,
        mesh=mesh,
        in_specs=(data, data, P("grp")) + (P(),) * 7,
        out_specs=P("grp", "frame", "row", None),
        check_vma=False,
    )
```

```python
import functools
import math

import jax
import jax.numpy as jnp
from jax import lax
from jax.experimental import pallas as pl
from jax.experimental.pallas import tpu as pltpu
from jax.sharding import PartitionSpec as P

HEAD_DIM = 72
HEADS = 8
STEPS = 1000
REACH = 2
STAGE = 8
HI = lax.Precision.HIGHEST
F32 = jnp.float32
MESH = pl.DeviceIdType.MESH


def noise_levels(timesteps):
    counter = jnp.arange(STEPS, dtype=F32)
    betas_all = 0.0001 + (0.02 - 0.0001) * counter / (STEPS - 1)
    log_keep = jnp.cumsum(jnp.log1p(-betas_all))
    selector = (jnp.arange(STEPS, dtype=jnp.int32)[None, :] == timesteps[:, None]).astype(F32)
    log_bar = jnp.dot(selector, log_keep, precision=HI)
    kept_share = jnp.exp(log_bar)
    return (jnp.sqrt(kept_share), jnp.sqrt(1.0 - kept_share))


def time_embed(timesteps, time_weight):
    halfway = time_weight.shape[0] // 2
    freqs_all = jnp.exp(-math.log(10000.0) * jnp.arange(halfway, dtype=F32) / halfway)
    angles = timesteps.astype(F32)[:, None] * freqs_all[None, :]
    features = jnp.concatenate([jnp.cos(angles), jnp.sin(angles)], axis=-1).astype(jnp.bfloat16)
    return jnp.dot(features, time_weight, preferred_element_type=F32)


def pieces(value, count):
    parts = []
    for _ in range(count):
        part = value.astype(jnp.bfloat16)
        parts.append(part)
        value = value - part.astype(F32)
    return parts


def wide_dot(value, weight, count=2):
    rows = value.shape[0]
    out = jnp.dot(jnp.concatenate(pieces(value, count), axis=0), weight, preferred_element_type=F32)
    return sum(out[i * rows : (i + 1) * rows] for i in range(count))


def centre(value):
    return value - jnp.mean(value, axis=-1, keepdims=True)


def local(
    latents,
    target_noise,
    timesteps,
    patch_weight,
    time_weight,
    spatial_project,
    spatial_output,
    temporal_project,
    temporal_output,
    final_weight,
):
    batches, frames_l, rows_l, cols, ch = latents.shape
    peers, halves = lax.axis_size("frame"), lax.axis_size("row")
    fi, gi = lax.axis_index("frame"), lax.axis_index("row")
    frames, rows = frames_l * peers, rows_l * halves
    places = rows_l * cols // peers
    q_rows, q_cols = max(1, places // cols), min(cols, places)
    width = patch_weight.shape[1]
    inner = spatial_output.shape[0]
    scale = 1.0 / math.sqrt(HEAD_DIM)

    signal, spread = noise_levels(timesteps)
    noisy = (
        signal[:, None, None, None, None] * latents
        + spread[:, None, None, None, None] * target_noise
    ).astype(jnp.bfloat16)
    time_vector = time_embed(timesteps, time_weight)

    whole = lax.all_gather(
        noisy.reshape(batches, frames_l, rows_l, cols * ch), ("frame", "row"), axis=0, tiled=False
    )
    whole = whole.reshape(peers, halves, batches, frames_l, rows_l, cols * ch)
    whole = whole.transpose(2, 0, 3, 1, 4, 5).reshape(batches, frames, rows, cols * ch)
    target = lax.all_to_all(
        target_noise.reshape(batches, frames_l, peers, places * ch),
        "frame",
        split_axis=2,
        concat_axis=1,
        tiled=True,
    ).reshape(batches * frames * places, ch)

    first = gi * rows_l + (fi * places) // cols
    column = (fi * places) % cols
    k_rows = q_rows + 2 * REACH
    padded = jnp.pad(whole, ((0, 0), (0, 0), (REACH, REACH), (0, 0)))
    near = lax.dynamic_slice_in_dim(padded, first, k_rows, axis=2).reshape(
        batches, frames, k_rows, cols, ch
    )
    own = lax.dynamic_slice_in_dim(near[:, :, REACH : REACH + q_rows], column, q_cols, axis=3)

    base = jnp.concatenate([patch_weight.astype(F32), time_vector], axis=0)
    base_c = centre(base)
    feats = base.shape[0]
    spatial = wide_dot(base_c, spatial_project, 3).reshape(feats, 3, HEADS, HEAD_DIM)
    mixer = jnp.einsum("ahe,bhe->hab", spatial[:, 0], spatial[:, 1], precision=HI) * scale
    out_heads = spatial_output.reshape(HEADS, HEAD_DIM, width).astype(F32)
    carried = jnp.einsum("ahe,hed->had", spatial[:, 2], out_heads, precision=HI)
    full_c = jnp.concatenate([base_c, centre(carried).reshape(HEADS * feats, width)], axis=0)
    temporal = wide_dot(full_c, temporal_project, 2)

    def lifted(tokens):
        mark = jnp.broadcast_to(
            jnp.eye(batches, dtype=F32)[:, None, None, None, :], tokens.shape[:-1] + (batches,)
        )
        return jnp.concatenate([tokens.astype(F32), mark], axis=-1)

    def scaled(tokens):
        stream = jnp.einsum("bfrca,ad->bfrcd", tokens, base_c, precision=HI)
        return tokens * lax.rsqrt(jnp.mean(stream * stream, axis=-1, keepdims=True) + 1e-06)

    near_l, own_l = lifted(near), lifted(own)
    keys = scaled(near_l).reshape(batches, frames, k_rows * cols, feats)
    query = scaled(own_l).reshape(batches, frames, places, feats)
    query = jnp.einsum("bfqa,hac->bfhqc", query, mixer, precision=HI)
    scores = jnp.einsum("bfhqc,bfkc->bfhqk", query, keys, precision=HI)
    key_row = jnp.arange(k_rows * cols, dtype=jnp.int32) // cols
    query_row = jnp.arange(places, dtype=jnp.int32) // q_cols
    off = key_row[None, :] - query_row[:, None]
    there = first + key_row - REACH
    inside = ((off >= 0) & (off <= 2 * REACH)) & ((there >= 0) & (there < rows))[None, :]
    scores = jnp.where(inside, scores, -1e30)
    exponent = jnp.exp(scores - jnp.max(scores, axis=-1, keepdims=True))
    weights = exponent / jnp.sum(exponent, axis=-1, keepdims=True)
    mixed = jnp.einsum("bfhqk,bfkc->bfqhc", weights, keys, precision=HI)
    tokens = batches * frames * places
    state = jnp.concatenate(
        [own_l.reshape(tokens, feats), mixed.reshape(tokens, HEADS * feats)], axis=-1
    )

    stream = jnp.dot(state, full_c, precision=HI)
    share = lax.rsqrt(jnp.mean(stream * stream, axis=-1, keepdims=True) + 1e-06)
    projected = (jnp.dot(state, temporal, precision=HI) * share).astype(jnp.bfloat16)
    shaped = projected.reshape(batches, frames, places, 3, HEADS, HEAD_DIM)
    scores = (
        jnp.einsum(
            "bfphe,bgphe->bphfg", shaped[:, :, :, 0], shaped[:, :, :, 1], preferred_element_type=F32
        )
        * scale
    )
    exponent = jnp.exp(scores - jnp.max(scores, axis=-1, keepdims=True))
    weights = (exponent / jnp.sum(exponent, axis=-1, keepdims=True)).astype(jnp.bfloat16)
    mixed = (
        jnp.einsum("bphfg,bgphe->bfphe", weights, shaped[:, :, :, 2], preferred_element_type=F32)
        .astype(jnp.bfloat16)
        .reshape(tokens, inner)
    )
    stream = stream + jnp.dot(mixed, temporal_output, preferred_element_type=F32)
    stream = centre(stream)
    share = lax.rsqrt(jnp.mean(stream * stream, axis=-1, keepdims=True) + 1e-06)
    predicted = jnp.dot(
        (stream * share).astype(jnp.bfloat16), final_weight, preferred_element_type=F32
    )
    gap = predicted - target
    errors = jnp.mean(gap * gap, axis=-1).reshape(batches, frames, places)
    errors = lax.all_to_all(errors, "frame", split_axis=1, concat_axis=2, tiled=True)
    return errors.reshape(batches, frames_l, rows_l, cols)


def dot(a, b, axes=((1,), (0,)), precision=None):
    return lax.dot_general(a, b, (axes, ((), ())), precision=precision, preferred_element_type=F32)


NT = ((1,), (1,))


def fused_kernel(
    peers,
    halves,
    times_ref,
    lat_ref,
    noise_ref,
    patch_ref,
    final_ref,
    tw_hbm,
    sp_hbm,
    so_hbm,
    tp_hbm,
    to_hbm,
    out_ref,
    tw,
    sp,
    so,
    tp,
    to,
    w_sem,
    x_ref,
    target_ref,
    near,
    goal,
    err_out,
    err_in,
    full,
    gt,
    state,
    stream1,
    qkv,
    mixed_t,
    x_send,
    x_recv,
    h_send,
    h_recv,
    t_send,
    t_recv,
    e_send,
    e_recv,
):
    batches, _, rows_l, ch, cols = lat_ref.shape
    lanes = x_ref.shape[-1]
    per = batches * cols
    pair = lanes // per
    width = patch_ref.shape[1]
    inner = so.shape[0]
    feats = ch + 8
    depth = full.shape[0]
    window = 2 * REACH + 1
    fi, gi = lax.axis_index("frame"), lax.axis_index("row")
    pairs = ((tw_hbm, tw), (sp_hbm, sp), (so_hbm, so), (tp_hbm, tp), (to_hbm, to))
    weight_copies = [
        pltpu.make_async_copy(src, dst, w_sem.at[i]) for i, (src, dst) in enumerate(pairs)
    ]
    for copy in weight_copies:
        copy.start()

    barrier = pltpu.get_barrier_semaphore()
    for df in range(peers):
        for dg in range(halves):
            if df or dg:
                pl.semaphore_signal(
                    barrier,
                    inc=1,
                    device_id={
                        "frame": lax.rem(fi + df, peers),
                        "row": lax.rem(gi + dg, halves),
                    },
                    device_id_type=MESH,
                )

    index = 128 * lax.broadcasted_iota(jnp.int32, (8, 128), 0) + lax.broadcasted_iota(
        jnp.int32, (8, 128), 1
    )
    logs = jnp.log1p(-(0.0001 + (0.02 - 0.0001) * index.astype(F32) / (STEPS - 1)))
    logs = jnp.where(index < STEPS, logs, 0.0)
    noisy = []
    for b in range(batches):
        kept = jnp.where(index <= times_ref[b], logs, 0.0)
        kept = jnp.exp(jnp.sum(jnp.sum(kept, axis=1, keepdims=True), axis=0, keepdims=True))
        signal, spread = jnp.sqrt(kept)[None], jnp.sqrt(1.0 - kept)[None]
        noisy.append(signal * lat_ref[b, 0] + spread * noise_ref[b, 0])
    blank = [jnp.zeros((rows_l, ch, lanes - per), F32)] if lanes > per else []
    rows = jnp.concatenate(noisy, axis=2)
    packed = window // 2 + 1
    empty = jnp.zeros((1, ch, per), F32)
    ahead = jnp.concatenate([rows[packed:], empty], axis=0)
    x_ref[0 : rows_l - packed + 1] = jnp.concatenate(
        [rows[: rows_l - packed + 1], ahead], axis=2
    ).astype(jnp.bfloat16)
    edges = ((rows_l - REACH, rows_l - REACH + 1), (0, 1))
    for i, (one, two) in enumerate(edges):
        x_ref[rows_l - packed + 1 + i] = jnp.concatenate(
            [rows[one], rows[two]], axis=1
        ).astype(jnp.bfloat16)
    target_ref[...] = jnp.concatenate(
        [noise_ref[b, 0] for b in range(batches)] + blank, axis=2
    )
    pl.semaphore_wait(barrier, peers * halves - 1)

    def start_of(place):
        return jnp.clip(place - REACH, 0, rows_l - window)

    def x_copy(peer):
        return pltpu.make_async_remote_copy(
            src_ref=x_ref.at[pl.ds(start_of(peer), packed)],
            dst_ref=near.at[fi, pl.ds(0, packed)],
            send_sem=x_send.at[peer],
            recv_sem=x_recv.at[fi],
            device_id={"frame": peer, "row": gi},
            device_id_type=MESH,
        )

    def t_copy(peer):
        return pltpu.make_async_remote_copy(
            src_ref=target_ref.at[peer],
            dst_ref=goal.at[fi],
            send_sem=t_send.at[peer],
            recv_sem=t_recv.at[fi],
            device_id={"frame": peer, "row": gi},
            device_id_type=MESH,
        )

    def halo_copy(slot, peer, half, first):
        return pltpu.make_async_remote_copy(
            src_ref=x_ref.at[first],
            dst_ref=near.at[fi, packed],
            send_sem=h_send.at[slot],
            recv_sem=h_recv.at[fi],
            device_id={"frame": peer, "row": half},
            device_id_type=MESH,
        )

    def halos(action):
        for i in range(REACH):

            @pl.when(gi < halves - 1)
            def _():
                action(halo_copy(i, i, gi + 1, rows_l - packed + 1))

            @pl.when(gi > 0)
            def _():
                action(halo_copy(REACH + i, peers - REACH + i, gi - 1, rows_l - packed + 2))

    for k in range(1, peers):
        x_copy(lax.rem(fi + k, peers)).start()
    halos(lambda copy: copy.start())
    near[fi, 0:packed] = x_ref[pl.ds(start_of(fi), packed)]
    goal[fi] = target_ref[fi]
    takes_halo = ((fi < REACH) & (gi > 0)) | ((fi >= peers - REACH) & (gi < halves - 1))

    @pl.when(jnp.logical_not(takes_halo))
    def _():
        near[:, packed:] = jnp.zeros((peers, 1, ch, lanes), near.dtype)

    halfway = tw.shape[0] // 2
    row = lax.broadcasted_iota(jnp.int32, (8, halfway), 0)
    place = lax.broadcasted_iota(jnp.int32, (8, halfway), 1)
    when = jnp.zeros((8, halfway), jnp.int32)
    for b in range(batches):
        when = jnp.where(row == b, times_ref[b], when)
    angles = when.astype(F32) * jnp.exp(-math.log(10000.0) * place.astype(F32) / halfway)
    used = row < batches
    features = jnp.concatenate(
        [jnp.where(used, jnp.cos(angles), 0.0), jnp.where(used, jnp.sin(angles), 0.0)], axis=1
    ).astype(jnp.bfloat16)
    weight_copies[0].wait()
    base = jnp.concatenate([patch_ref[...].astype(F32), dot(features, tw[...])], axis=0)
    base_c = base - jnp.mean(base, axis=-1, keepdims=True)
    b1, b2, b3 = pieces(base_c, 3)
    weight_copies[1].wait()
    wide = dot(jnp.concatenate([b1, b2, b3], axis=0), sp[...], NT)
    spatial = wide[:feats] + wide[feats : 2 * feats] + wide[2 * feats :]
    sq, sk, sv = (spatial[:, i * inner : (i + 1) * inner] for i in range(3))
    owner = lax.broadcasted_iota(jnp.int32, (feats, inner), 1) // HEAD_DIM

    def by_head(value):
        return jnp.concatenate(
            [jnp.where(owner == h, value, 0.0) for h in range(HEADS)], axis=0
        )

    sk3 = jnp.concatenate([sk] * 3 + [jnp.zeros((128 - 3 * feats, inner), F32)], axis=0)
    mixer = dot(by_head(sq), sk3, NT, HI) * (1.0 / math.sqrt(HEAD_DIM))
    mixer = jnp.concatenate(
        [mixer[h * feats : (h + 1) * feats] for h in range(HEADS)], axis=1
    )
    mixer = jnp.concatenate(pieces(mixer, 3), axis=0)
    v1, v2 = pieces(by_head(sv), 2)
    weight_copies[2].wait()
    carried = dot(v1, so[...]) + dot(v2, so[...])
    carried = carried - jnp.mean(carried, axis=-1, keepdims=True)
    rest = depth - feats * (HEADS + 2)
    full[...] = jnp.concatenate(
        [base_c, carried, base_c - b1.astype(F32), jnp.zeros((rest, width), F32)], axis=0
    ).astype(jnp.bfloat16)
    small = dot(base_c, base_c, NT, HI) * (1.0 / width)
    small = jnp.concatenate(pieces(small, 3), axis=0)
    for k in range(1, peers):
        t_copy(lax.rem(fi + k, peers)).start()
    weight_copies[3].wait()
    turned_full = dot(tp[...], full[...], NT)
    scale = 1.0 / math.sqrt(HEAD_DIM)
    gt[0:inner] = (turned_full[:inner] * scale).astype(jnp.bfloat16)
    gt[inner:] = turned_full[inner:].astype(jnp.bfloat16)

    for k in range(1, peers):
        other = lax.rem(fi + k, peers)
        x_copy(other).wait_send()
        pltpu.make_async_remote_copy(
            src_ref=x_ref.at[pl.ds(0, packed)],
            dst_ref=near.at[other, pl.ds(0, packed)],
            send_sem=x_send.at[other],
            recv_sem=x_recv.at[other],
            device_id={"frame": other, "row": gi},
            device_id_type=MESH,
        ).wait_recv()
    halos(lambda copy: copy.wait_send())

    @pl.when(takes_halo)
    def _():
        for k in range(peers):
            pltpu.make_async_remote_copy(
                src_ref=x_ref.at[0],
                dst_ref=near.at[k, packed],
                send_sem=h_send.at[0],
                recv_sem=h_recv.at[k],
                device_id={"frame": k, "row": lax.rem(gi + 1, halves)},
                device_id_type=MESH,
            ).wait_recv()

    span = -(-window * cols // lanes) * lanes
    spots = []
    key_lane = lax.broadcasted_iota(jnp.int32, (1, span), 1)
    bias = jnp.full((1, span), -1e30, F32)
    for d in range(-REACH, REACH + 1):
        lr = fi + d
        outside = (lr < 0) | (lr >= rows_l)
        step = jnp.where(lr < 0, lr + REACH, jnp.where(lr >= rows_l, lr - rows_l, lr - start_of(fi)))
        second = jnp.where(outside, step == 1, step >= packed)
        entry = jnp.where(outside, packed, jnp.where(step >= packed, step - packed, step))
        spots.append((entry, second))
        there = gi * rows_l + lr
        level = jnp.where((there >= 0) & (there < rows_l * halves), 0.0, -1e30).astype(F32)
        bias = jnp.where(key_lane // cols == d + REACH, level, bias)

    tail = [jnp.zeros((ch, span - window * cols), F32)] if span > window * cols else []
    groups, owns = [], []
    for f in range(peers):
        seen = [near[f, entry].astype(F32) for entry, _ in spots]
        seen = [
            jnp.where(second, v[:, per:], v[:, :per]) for v, (_, second) in zip(seen, spots)
        ]
        owns.append(seen[REACH])
        for b in range(batches):
            groups.append(
                jnp.concatenate([v[:, b * cols : (b + 1) * cols] for v in seen] + tail, axis=1)
            )

    def lifted(value, video):
        mark = (
            video == lax.broadcasted_iota(jnp.int32, (feats - ch, value.shape[1]), 0)
        ).astype(F32)
        return jnp.concatenate([value, mark], axis=0)

    def spread_of(value):
        part = dot(small, value.astype(jnp.bfloat16))
        part = part[:feats] + part[feats : 2 * feats] + part[2 * feats :]
        var = jnp.sum(value * part, axis=0, keepdims=True)
        return lax.rsqrt(jnp.maximum(var, 0.0) + 1e-06)

    own = jnp.concatenate(owns, axis=1)
    tokens = own.shape[1]
    video = lax.broadcasted_iota(jnp.int32, (feats - ch, tokens), 1) % per // cols
    own = lifted(own, video)
    state[0:feats, :] = own
    state[feats * (HEADS + 1) : feats * (HEADS + 2), :] = own
    state[feats * (HEADS + 2) :, :] = jnp.zeros((rest, tokens), F32)
    turned_own = jnp.concatenate(
        [own] * 3 + [jnp.broadcast_to(spread_of(own), (128 - 3 * feats, tokens))], axis=0
    ).T
    ask = dot(turned_own[:, : 3 * feats].astype(jnp.bfloat16), mixer)
    ask = ask * turned_own[:, 3 * feats : 3 * feats + 1]
    lead = ask.astype(jnp.bfloat16).astype(F32)
    lane = lax.broadcasted_iota(jnp.int32, ask.shape, 1) % 128
    ask3 = jnp.where(lane < 2 * feats, lead, ask - lead)
    ask3 = jnp.where(lane == 3 * feats, 1.0, ask3).astype(jnp.bfloat16)

    count = len(groups)
    near_all = jnp.concatenate(groups, axis=1)
    video = lax.broadcasted_iota(jnp.int32, (feats - ch, count * span), 1) // span % batches
    near_all = lifted(near_all, video)
    y = near_all * spread_of(near_all)
    high = y.astype(jnp.bfloat16).astype(F32)
    low = y - high
    blocked = jnp.concatenate([bias] * count, axis=1)
    keys3 = jnp.concatenate(
        [high, low, high, blocked, jnp.zeros((127 - 3 * feats, count * span), F32)], axis=0
    ).astype(jnp.bfloat16)
    values = jnp.concatenate([high, low, jnp.ones((16, count * span), F32)], axis=0)
    values = values.astype(jnp.bfloat16)
    tiles_of_u = []
    for first in range(0, count, STAGE):
        some = range(first, min(first + STAGE, count))
        scores = [
            dot(
                jnp.concatenate(
                    [
                        ask3[g * cols : (g + 1) * cols, h * 128 : (h + 1) * 128]
                        for h in range(HEADS)
                    ],
                    axis=0,
                ),
                keys3[:, g * span : (g + 1) * span],
            )
            for g in some
        ]
        tops = [jnp.max(v, axis=1, keepdims=True) for v in scores]
        weights = [jnp.exp(v - t).astype(jnp.bfloat16) for v, t in zip(scores, tops)]
        sums = [
            dot(values[:, g * span : (g + 1) * span], w, NT) for g, w in zip(some, weights)
        ]
        tiles_of_u += [
            (v[:feats] + v[feats : 2 * feats]) * (1.0 / v[2 * feats : 2 * feats + 1])
            for v in sums
        ]
    for h in range(HEADS):
        state[feats * (h + 1) : feats * (h + 2), :] = jnp.concatenate(
            [u[:, h * cols : (h + 1) * cols] for u in tiles_of_u], axis=1
        )

    z = state[...]
    z = z.astype(jnp.bfloat16)
    stream1[...] = dot(z.T, full[...])
    square = stream1[...]
    square = (square * square).astype(jnp.bfloat16)
    var = dot(jnp.ones((16, width), jnp.bfloat16), square, NT)[0:1] * (1.0 / width)
    qkv[...] = dot(gt[...], z) * lax.rsqrt(var + 1e-06)
    tiles = peers // pair

    def tile_of(part, h, t):
        top = part * inner + h * HEAD_DIM
        return qkv[top : top + HEAD_DIM, t * lanes : (t + 1) * lanes]

    def turned(value, s):
        return pltpu.roll(value, s * per, 1) if s else value

    shifts = [(t, s) for t in range(tiles) for s in range(pair)]
    logits = [[[] for _ in shifts] for _ in range(tiles)]
    for h in range(HEADS):
        ks = [turned(tile_of(1, h, t), s) for t, s in shifts]
        for p in range(tiles):
            q = tile_of(0, h, p)
            for slot, k in zip(logits[p], ks):
                slot.append(jnp.sum(q * k, axis=0, keepdims=True))
    shares = []
    for p in range(tiles):
        rows = [jnp.concatenate(slot, axis=0) for slot in logits[p]]
        top = functools.reduce(jnp.maximum, rows)
        exps = [jnp.exp(v - top) for v in rows]
        total = 1.0 / functools.reduce(jnp.add, exps)
        shares.append([e * total for e in exps])
    for h in range(HEADS):
        vs = [turned(tile_of(2, h, t), s) for t, s in shifts]
        for p in range(tiles):
            mixed_t[h * HEAD_DIM : (h + 1) * HEAD_DIM, p * lanes : (p + 1) * lanes] = (
                functools.reduce(jnp.add, [w[h : h + 1] * v for w, v in zip(shares[p], vs)])
            )

    weight_copies[4].wait()
    stream = stream1[...] + dot(mixed_t[...].astype(jnp.bfloat16).T, to[...])
    stream = stream - jnp.mean(stream, axis=-1, keepdims=True)
    share = lax.rsqrt(jnp.mean(stream * stream, axis=-1, keepdims=True) + 1e-06)
    predicted = dot(final_ref[...], (stream * share).astype(jnp.bfloat16), NT)

    for k in range(1, peers):
        other = lax.rem(fi + k, peers)
        t_copy(other).wait_send()
        pltpu.make_async_remote_copy(
            src_ref=target_ref.at[0],
            dst_ref=goal.at[other],
            send_sem=t_send.at[other],
            recv_sem=t_recv.at[other],
            device_id={"frame": other, "row": gi},
            device_id_type=MESH,
        ).wait_recv()
    aim = jnp.concatenate([goal[f][:, :per] for f in range(peers)], axis=1)
    gap = predicted - aim
    errors = jnp.sum(gap * gap, axis=0, keepdims=True)
    for t in range(tiles):
        err_out[t] = jnp.broadcast_to(errors[:, t * lanes : (t + 1) * lanes], (8, lanes))

    def e_copy(peer, source, other):
        return pltpu.make_async_remote_copy(
            src_ref=err_out.at[peer // pair],
            dst_ref=err_in.at[source],
            send_sem=e_send.at[peer],
            recv_sem=e_recv.at[source],
            device_id={"frame": other, "row": gi},
            device_id_type=MESH,
        )

    for k in range(1, peers):
        other = lax.rem(fi + k, peers)
        e_copy(other, fi, other).start()
    err_in[fi] = err_out[fi // pair]
    for k in range(1, peers):
        other = lax.rem(fi + k, peers)
        e_copy(other, fi, other).wait_send()
        e_copy(fi, other, other).wait_recv()
    got = jnp.concatenate([err_in[k, 0:1] for k in range(peers)], axis=0)
    result = got[:, :per]
    for s in range(1, pair):
        result = jnp.where(lax.rem(fi, pair) == s, got[:, s * per : (s + 1) * per], result)
    for b in range(batches):
        out_ref[b, 0] = result[:, b * cols : (b + 1) * cols]


def fused(
    latents,
    target_noise,
    timesteps,
    patch_weight,
    time_weight,
    spatial_project,
    spatial_output,
    temporal_project,
    temporal_output,
    final_weight,
):
    batches, frames_l, rows_l, cols, ch = latents.shape
    peers, halves = lax.axis_size("frame"), lax.axis_size("row")
    width, inner = patch_weight.shape[1], spatial_output.shape[0]
    per, lanes = batches * cols, 128
    feats = ch + 8
    tokens = peers * per
    depth = -(-(feats * (HEADS + 2)) // 128) * 128
    bf16 = jnp.bfloat16
    vmem, anywhere = pl.BlockSpec(memory_space=pltpu.VMEM), pl.BlockSpec(memory_space=pl.ANY)
    smem = pl.BlockSpec(memory_space=pltpu.SMEM)
    sems = pltpu.SemaphoreType.DMA
    summed = pl.pallas_call(
        functools.partial(fused_kernel, peers, halves),
        out_shape=jax.ShapeDtypeStruct((batches, frames_l, rows_l, cols), F32),
        in_specs=[smem] + [vmem] * 4 + [anywhere] * 5,
        out_specs=vmem,
        scratch_shapes=[
            pltpu.VMEM(time_weight.shape, bf16),
            pltpu.VMEM(spatial_project.shape[::-1], bf16),
            pltpu.VMEM(spatial_output.shape, bf16),
            pltpu.VMEM(temporal_project.shape[::-1], bf16),
            pltpu.VMEM(temporal_output.shape, bf16),
            sems((5,)),
            pltpu.VMEM((rows_l, ch, lanes), bf16),
            pltpu.VMEM((rows_l, ch, lanes), F32),
            pltpu.VMEM((peers, REACH + 2, ch, lanes), bf16),
            pltpu.VMEM((peers, ch, lanes), F32),
            pltpu.VMEM((tokens // lanes, 8, lanes), F32),
            pltpu.VMEM((peers, 8, lanes), F32),
            pltpu.VMEM((depth, width), bf16),
            pltpu.VMEM((3 * inner, depth), bf16),
            pltpu.VMEM((depth, tokens), F32),
            pltpu.VMEM((tokens, width), F32),
            pltpu.VMEM((3 * inner, tokens), F32),
            pltpu.VMEM((inner, tokens), F32),
            sems((peers,)),
            sems((peers,)),
            sems((2 * REACH,)),
            sems((peers,)),
            sems((peers,)),
            sems((peers,)),
            sems((peers,)),
            sems((peers,)),
        ],
        compiler_params=pltpu.CompilerParams(
            collective_id=0, has_side_effects=True, vmem_limit_bytes=56 * 1024 * 1024
        ),
        cost_estimate=pl.CostEstimate(
            flops=4 * 10**9, bytes_accessed=11 * 10**6, transcendentals=10**6
        ),
    )(
        timesteps,
        latents.transpose(0, 1, 2, 4, 3),
        target_noise.transpose(0, 1, 2, 4, 3),
        patch_weight,
        final_weight.T,
        time_weight,
        spatial_project.T,
        spatial_output,
        temporal_project.T,
        temporal_output,
    )
    return summed * (1.0 / ch)


def fits(latents):
    batches, frames_l, rows_l, cols, ch = latents.shape
    per = batches * cols
    return (
        frames_l == 1
        and rows_l == lax.axis_size("frame")
        and rows_l >= 3 * REACH
        and 2 * per == 128
        and REACH == 2
        and (rows_l * per) % 128 == 0
        and ch % 16 == 0
        and batches <= 8
        and 3 * (ch + 8) < 128
    )


def choose(latents, target_noise, timesteps, *weights):
    plan = fused if fits(latents) else local
    return plan(latents, target_noise, timesteps, *weights)


def solution(mesh):
    data = P("grp", "frame", "row", None, None)
    return jax.shard_map(
        choose,
        mesh=mesh,
        in_specs=(data, data, P("grp")) + (P(),) * 7,
        out_specs=P("grp", "frame", "row", None),
        check_vma=False,
    )
```
